256 devices in a mesh: seq: 16 (over x_lo, y, core), head: 8 (over z), batch: 2 (over x_hi).
Axes of the slice: x: 4 (x_hi: 2, x_lo: 2; x = x_hi * 2 + x_lo), y: 4, z: 8, core: 2. Of those that a mesh axis runs over, the one named last changes fastest.
Arguments:
- query_vectors: bfloat16 [4, 16384, 2048], P('batch', 'seq', 'head'), parts along dimension 0, may hold values from -6 to 6
- key_vectors: bfloat16 [4, 16384, 2048], P('batch', 'seq', 'head'), parts along dimension 0, may hold values from -6 to 6
- value_vectors: bfloat16 [4, 16384, 2048], P('batch', 'seq', 'head'), parts along dimension 0, may hold values from -6 to 6
- token_rates: float32 [4, 16, 16384], P('batch', 'head', 'seq'), parts along dimension 0, may hold values from 0.05 to 1
- gate_weight: float32 [16, 128, 256], P('head'), may hold values from -0.5 to 0.5
- up_weight: float32 [16, 128, 256], P('head'), may hold values from -0.5 to 0.5
- down_weight: float32 [16, 128, 256], P('head'), may hold values from -0.375 to 0.375
- step_sizes: float32 [16], P('head'), may hold values from 0.3 to 1
- norm_gain: float32 [2048], P('head'), may hold values from 0.1 to 1.9
Outputs:
- mixed: bfloat16 [4, 16384, 2048], P('batch', 'seq', 'head'), parts along dimension 0
- final_weights: float32 [6, 16, 128, 256], P('batch', 'head'), parts along dimension 0
The draws below stay inside these ranges and needn't reach their ends.
There are 2 independent parts, one for each index of `batch`. The reference program is written for one: setup_inputs(seed, part) draws one part's arguments, and reference() takes and returns one part's arrays. A program takes and returns all parts, laid end to end along the dimension named above; an argument that names none is the same for every part. Nothing has to cross between parts.
All inputs are finite; a program needn't handle non-finite values.
Results may differ from the reference program's by a relative error of at most 0.008.
Values may be sent and summed in bfloat16 or wider, within the bound.
No kernel may reach another device: no remote copies, remote signals or barrier semaphores. Data moves between devices by JAX's collectives and lax.ppermute only.
A program may use at most 128 MiB of HBM per device.

```python
import math
import jax
import jax.numpy as jnp
from jax import lax

HD = 128
FW = 256
HEADS = 16
TOK_DEV = 1024
GROUPS = 2
NS_STEPS = 5
GROUP = 16384
WINDOW = 2048


def drawn_pair(key):
    shape = (GROUPS, GROUP, HEADS * HD)
    first, second = jax.random.split(jax.random.fold_in(key, 4242), 2)
    query_draw = jax.random.truncated_normal(first, -5.5, 5.5, shape, jnp.float32)
    key_draw = jax.random.truncated_normal(second, -5.5, 5.5, shape, jnp.float32)
    return (query_draw.astype(jnp.bfloat16), key_draw.astype(jnp.bfloat16))


def draw_query_vectors(key, part):
    return drawn_pair(key)[0]


def draw_key_vectors(key, part):
    return drawn_pair(key)[1]


def level_of(key, dims, shards, least, top_value):
    factor_of, own = 1.0, jax.random.fold_in(key, 6)
    for axis_at, shards_of in shards:
        draws = jnp.exp(jax.random.uniform(jax.random.fold_in(own, axis_at), (shards_of,), jnp.float32, least / len(shards), top_value / len(shards)))
        factor_of = factor_of * jnp.repeat(draws, dims[axis_at] // shards_of).reshape([-1 if axis == axis_at else 1 for axis in range(len(dims))])
    return factor_of


def scatter_about(key, shape, scale, most, shards=(), held_as=jnp.bfloat16):
    factor_of = level_of(key, shape, shards, -0.22, 0.18) if shards else 1.0
    entries = jax.random.normal(key, shape, jnp.float32) * scale * factor_of
    return jnp.minimum(jnp.maximum(entries, -most), most).astype(held_as)


def setup_inputs(seed: int = 0, part: int = 0) -> dict:
    key_of = jax.random.split(jax.random.key(seed), 10)
    own_keys = jax.random.split(jax.random.fold_in(key_of[9], part), 10)
    query_vectors = draw_query_vectors(jax.random.fold_in(jax.random.fold_in(key_of[9], part), 71), part)
    key_vectors = draw_key_vectors(jax.random.fold_in(jax.random.fold_in(key_of[9], part), 71), part)
    value_vectors = scatter_about(own_keys[2], (GROUPS, GROUP, HEADS * HD), 1.0, 6.0, ((1, 16), (2, 8)))
    token_rates = jnp.clip(jnp.exp(math.log(1.0) - 2.9957323 * jax.random.uniform(own_keys[3], (GROUPS, HEADS, GROUP), jnp.float32) ** level_of(own_keys[3], (GROUPS, HEADS, GROUP), ((1, 8), (2, 16)), -0.2, 0.2)), 0.05, 1.0)
    gate_weight = scatter_about(key_of[4], (HEADS, HD, FW), HD ** -0.5, 0.5, ((0, 8),), jnp.float32)
    up_weight = scatter_about(key_of[5], (HEADS, HD, FW), HD ** -0.5, 0.5, ((0, 8),), jnp.float32)
    down_weight = scatter_about(key_of[6], (HEADS, HD, FW), FW ** -0.5, 0.375, ((0, 8),), jnp.float32)
    step_sizes = jnp.clip(jnp.exp(math.log(1.0) - 1.2039728 * jax.random.uniform(key_of[7], (HEADS,), jnp.float32) ** level_of(key_of[7], (HEADS,), ((0, 8),), -0.2, 0.2)), 0.3, 1.0)
    norm_gain = jnp.clip(1.0 + 0.18 * jax.random.normal(key_of[8], (HEADS * HD,), jnp.float32), 0.1, 1.9)
    return {"query_vectors": query_vectors, "key_vectors": key_vectors, "value_vectors": value_vectors, "token_rates": token_rates, "gate_weight": gate_weight, "up_weight": up_weight, "down_weight": down_weight, "step_sizes": step_sizes, "norm_gain": norm_gain}


coeff_first = 3.4445
coeff_second = -4.775
coeff_third = 2.0315
frob_epsilon = 1e-07
rms_epsilon = 1e-06
column_epsilon = 1e-06

def fast_forward(inputs, w_gate, w_up):
    gate_pre = jnp.dot(inputs, w_gate.astype(jnp.bfloat16), preferred_element_type=jnp.float32)
    up_pre = jnp.dot(inputs, w_up.astype(jnp.bfloat16), preferred_element_type=jnp.float32)
    squash = jax.nn.sigmoid(gate_pre)
    active = gate_pre * squash
    hidden_act = (active * up_pre).astype(jnp.bfloat16)
    return (gate_pre, up_pre, squash, active, hidden_act)

def fast_apply(items):
    queries, w_gate, w_up, w_down = items
    hidden_act = fast_forward(queries, w_gate, w_up)[4]
    return jnp.dot(hidden_act, w_down.astype(jnp.bfloat16).T, preferred_element_type=jnp.float32)

def fast_grads(items):
    key_rows, value_rows, rate_rows, w_gate, w_up, w_down = items
    gate_pre, up_pre, squash, active, hidden_act = fast_forward(key_rows, w_gate, w_up)
    out_grad = (-rate_rows[:, None] * value_rows.astype(jnp.float32)).astype(jnp.bfloat16)
    grad_down = jnp.dot(out_grad.T, hidden_act, preferred_element_type=jnp.float32)
    hidden_grad = jnp.dot(out_grad, w_down.astype(jnp.bfloat16), preferred_element_type=jnp.float32)
    up_grad = (hidden_grad * active).astype(jnp.bfloat16)
    gate_grad = (hidden_grad * up_pre * squash * (1.0 + gate_pre * (1.0 - squash))).astype(jnp.bfloat16)
    grad_gate = jnp.dot(key_rows.T, gate_grad, preferred_element_type=jnp.float32)
    grad_up = jnp.dot(key_rows.T, up_grad, preferred_element_type=jnp.float32)
    return (grad_gate, grad_up, grad_down)

def orthogonalize(gradient):
    matrix = gradient / (jnp.sqrt(jnp.sum(gradient * gradient)) + frob_epsilon)
    for sweep in range(NS_STEPS):
        gram_matrix = jnp.dot(matrix, matrix.T, precision=lax.Precision.HIGHEST)
        polynomial = coeff_second * gram_matrix + coeff_third * jnp.dot(gram_matrix, gram_matrix, precision=lax.Precision.HIGHEST)
        matrix = coeff_first * matrix + jnp.dot(polynomial, matrix, precision=lax.Precision.HIGHEST)
    return matrix

def renew(weight, gradient, step_rate, target):
    stepped = weight - step_rate * orthogonalize(gradient)
    length = jnp.sqrt(lax.optimization_barrier(jnp.sum(stepped * stepped, axis=0)))
    return stepped * (target / (length + column_epsilon))

def window_attention(queries, key_rows, value_rows):
    row_count = queries.shape[0]
    block_rows = min(512, TOK_DEV)
    scale = 1.0 / math.sqrt(HD)
    front_pad = jnp.zeros((WINDOW, HEADS, HD), jnp.bfloat16)
    keys_padded = jnp.concatenate([front_pad, key_rows], axis=0)
    values_padded = jnp.concatenate([front_pad, value_rows], axis=0)

    def one_block(block_index):
        first_row = (block_index * block_rows).astype(jnp.int32)
        query_block = lax.dynamic_slice_in_dim(queries, first_row, block_rows, 0).astype(jnp.float32)
        key_block = lax.dynamic_slice_in_dim(keys_padded, first_row, WINDOW + block_rows, 0).astype(jnp.float32)
        value_block = lax.dynamic_slice_in_dim(values_padded, first_row, WINDOW + block_rows, 0).astype(jnp.float32)
        scores = jnp.einsum('qhd,khd->hqk', query_block, key_block) * scale
        offset = jnp.arange(block_rows, dtype=jnp.int32)[:, None] - jnp.arange(WINDOW + block_rows, dtype=jnp.int32)[None, :] + WINDOW
        key_place = first_row - WINDOW + jnp.arange(WINDOW + block_rows, dtype=jnp.int32)
        allowed = (offset >= 0) & (offset < WINDOW) & (key_place[None, :] >= 0)
        scores = jnp.where(allowed[None], scores, -jnp.inf)
        row_max = lax.optimization_barrier(jnp.max(scores, axis=-1, keepdims=True))
        raised = jnp.exp(scores - row_max)
        attend = (raised / lax.optimization_barrier(jnp.sum(raised, axis=-1, keepdims=True))).astype(jnp.bfloat16)
        return jnp.einsum('hqk,khd->qhd', attend.astype(jnp.float32), value_block)
    blocks_out = lax.map(one_block, jnp.arange(row_count // block_rows, dtype=jnp.int32))
    return blocks_out.reshape(row_count, HEADS, HD)

def reference(query_vectors, key_vectors, value_vectors, token_rates, gate_weight, up_weight, down_weight, step_sizes, norm_gain):
    attended = window_attention(query_vectors.reshape(GROUPS * GROUP, HEADS, HD), key_vectors.reshape(GROUPS * GROUP, HEADS, HD), value_vectors.reshape(GROUPS * GROUP, HEADS, HD))
    attended = attended.reshape(GROUPS, GROUP, HEADS, HD)
    weights = (gate_weight, up_weight, down_weight)
    targets = tuple((jnp.sqrt(lax.optimization_barrier(jnp.sum(matrix_in * matrix_in, axis=1))) for matrix_in in weights))
    gain = norm_gain.reshape(HEADS, HD)
    mixed_groups = []
    for group in range(GROUPS):
        query_group = query_vectors[group].reshape(GROUP, HEADS, HD).transpose(1, 0, 2)
        key_group = key_vectors[group].reshape(GROUP, HEADS, HD).transpose(1, 0, 2)
        value_group = value_vectors[group].reshape(GROUP, HEADS, HD).transpose(1, 0, 2)
        applied = lax.map(fast_apply, (query_group,) + weights).transpose(1, 0, 2)
        normed = applied * lax.rsqrt(lax.optimization_barrier(jnp.mean(applied * applied, axis=-1, keepdims=True)) + rms_epsilon) * gain
        mixed_groups.append((normed + attended[group]).astype(jnp.bfloat16).reshape(GROUP, HEADS * HD))
        gradients = lax.map(fast_grads, (key_group, value_group, token_rates[group]) + weights)
        weights = tuple((jax.vmap(renew)(weights[which], gradients[which], step_sizes, targets[which]) for which in range(3)))
    return (jnp.stack(mixed_groups), jnp.stack(weights))
```

```python
import functools
import math

import jax
import jax.numpy as jnp
from jax import lax
from jax.experimental import pallas as pl
from jax.experimental.pallas import tpu as pltpu
from jax.sharding import PartitionSpec as P

HD = 128
FW = 256
NS_STEPS = 5
ROWS = 256

coeff_first = 3.4445
coeff_second = -4.775
coeff_third = 2.0315
frob_epsilon = 1e-07
rms_epsilon = 1e-06
column_epsilon = 1e-06

f32 = jnp.float32
bf16 = jnp.bfloat16
LEAST_SUM = 1e-25
MOST_SUM = 1e30
VMEM_LIMIT = 48 * 1024 * 1024


def dot(a, b, over=((1,), (0,))):
    return lax.dot_general(a, b, (over, ((), ())), preferred_element_type=f32)


def sigmoid(x):
    return 0.5 * jnp.tanh(0.5 * x) + 0.5


def move(block, route):
    return lax.ppermute(block, "seq", [(i, route(i)) for i in range(lax.axis_size("seq"))])


def grads_kernel(k_ref, v_ref, r_ref, wg_ref, wu_ref, wd_ref, out_ref, grad_ref, hid_ref, og_ref):
    tokens = k_ref.shape[0]
    heads = r_ref.shape[0]
    for h in range(heads):
        lanes = slice(h * HD, (h + 1) * HD)
        low_gate = wg_ref[h].astype(bf16)
        low_up = wu_ref[h].astype(bf16)
        low_down = wd_ref[h].astype(bf16)
        for c in range(tokens // ROWS):
            rows = slice(c * ROWS, (c + 1) * ROWS)
            keys = k_ref[rows, lanes]
            rate = jnp.broadcast_to(r_ref[h : h + 1, rows], (HD, ROWS)).T
            out_grad = (-rate * v_ref[rows, lanes].astype(f32)).astype(bf16)
            gate_pre = dot(keys, low_gate)
            up_pre = dot(keys, low_up)
            hidden_grad = dot(out_grad, low_down)
            sig = sigmoid(gate_pre)
            active = gate_pre * sig
            og_ref[rows] = out_grad
            hid_ref[rows] = (active * up_pre).astype(bf16)
            grad_ref[rows, FW:] = (hidden_grad * active).astype(bf16)
            grad_ref[rows, :FW] = (
                hidden_grad * up_pre * sig * (1.0 + gate_pre * (1.0 - sig))
            ).astype(bf16)
        both = dot(k_ref[:, lanes], grad_ref[...], ((0,), (0,)))
        down = dot(og_ref[...], hid_ref[...], ((0,), (0,)))
        for which, full in enumerate((both[:, :FW], both[:, FW:], down)):
            for half in range(2):
                out_ref[(which * heads + h) * 2 + half] = full[
                    :, half * HD : (half + 1) * HD
                ].astype(out_ref.dtype)


def local_grads(keys, values, rates, weights):
    tokens, width = keys.shape
    heads = width // HD
    vmem = pl.BlockSpec(memory_space=pltpu.VMEM)
    return pl.pallas_call(
        grads_kernel,
        out_shape=jax.ShapeDtypeStruct((6 * heads, HD, HD), bf16),
        in_specs=[vmem] * 6,
        out_specs=vmem,
        scratch_shapes=[
            pltpu.VMEM((tokens, 2 * FW), bf16),
            pltpu.VMEM((tokens, FW), bf16),
            pltpu.VMEM((tokens, HD), bf16),
        ],
        compiler_params=pltpu.CompilerParams(vmem_limit_bytes=VMEM_LIMIT),
        cost_estimate=pl.CostEstimate(
            flops=12 * heads * tokens * HD * FW,
            bytes_accessed=4 * tokens * width,
            transcendentals=heads * tokens * FW,
        ),
        name="local_grads",
    )(keys, values, rates, *weights)


def split(x):
    high = x.astype(bf16)
    return high, (x - high.astype(f32)).astype(bf16)


def step_kernel(step_ref, s_ref, *refs):
    w_refs, first_refs, out_refs, x_ref = refs[:3], refs[3:6], refs[6:9], refs[9]
    heads = w_refs[0].shape[0]
    count = 3 * heads
    for m in range(count):
        grad = jnp.concatenate([s_ref[2 * m], s_ref[2 * m + 1]], axis=1).astype(f32)
        frobenius = jnp.sqrt(jnp.sum(grad * grad, keepdims=True))
        x_ref[m] = grad / (frobenius + frob_epsilon)

    def sweep(_, carry):
        pieces, polynomials = [], []
        for m in range(count):
            high, low = split(x_ref[m])
            pieces.append((high, low))
            stacked = jnp.concatenate([high, low], axis=0)
            g = dot(stacked, stacked, ((1,), (1,)))
            gram = g[:HD, :HD] + (g[HD:, :HD] + g[:HD, HD:]) + g[HD:, HD:]
            g_high, g_low = split(gram)
            row = jnp.concatenate([g_high, g_low], axis=1)
            squared = dot(row, jnp.concatenate([row, row], axis=0))
            polynomials.append(
                coeff_second * gram + coeff_third * (squared[:, :HD] + squared[:, HD:])
            )
        for m in range(count):
            high, low = pieces[m]
            row = jnp.concatenate(split(polynomials[m]), axis=1)
            product = dot(row, jnp.concatenate([high, high], axis=0)) + dot(
                row, jnp.concatenate([low, low], axis=0)
            )
            x_ref[m] = coeff_first * x_ref[m] + product
        return carry

    lax.fori_loop(0, NS_STEPS, sweep, 0)
    for which in range(3):
        for h in range(heads):
            first = first_refs[which][h]
            target = jnp.sqrt(jnp.sum(first * first, axis=0, keepdims=True))
            stepped = w_refs[which][h] - step_ref[h] * x_ref[which * heads + h]
            length = jnp.sqrt(jnp.sum(stepped * stepped, axis=0, keepdims=True))
            out_refs[which][h] = stepped * (target / (length + column_epsilon))


def step(summed, weights, first, step_sizes):
    heads = weights[0].shape[0]
    vmem = pl.BlockSpec(memory_space=pltpu.VMEM)
    return pl.pallas_call(
        step_kernel,
        out_shape=[jax.ShapeDtypeStruct(w.shape, f32) for w in weights],
        in_specs=[pl.BlockSpec(memory_space=pltpu.SMEM)] + [vmem] * 7,
        out_specs=[vmem] * 3,
        scratch_shapes=[pltpu.VMEM((3 * heads, HD, FW), f32)],
        compiler_params=pltpu.CompilerParams(vmem_limit_bytes=VMEM_LIMIT),
        cost_estimate=pl.CostEstimate(
            flops=3 * heads * NS_STEPS * 40 * HD * HD * FW,
            bytes_accessed=3 * heads * 10 * HD * FW,
            transcendentals=0,
        ),
        name="weight_step",
    )(step_sizes, summed, *weights, *first)


def mix_kernel(
    first_group,
    rank_ref,
    q_ref,
    ko_ref,
    vo_ref,
    kn_ref,
    vn_ref,
    kf_ref,
    vf_ref,
    wg_ref,
    wu_ref,
    wd_ref,
    gain_ref,
    out_ref,
    wide_own,
    wide_near,
    wide_far,
    attended_ref,
):
    tokens = q_ref.shape[0]
    scale = 1.0 / math.sqrt(HD)
    power = scale * math.log2(math.e)
    blocks = tokens // ROWS
    ones = jnp.ones((ROWS, HD), bf16)
    near_valid = rank_ref[0] >= 1 if first_group else True
    far_valid = rank_ref[0] >= 2 if first_group else True
    for wide, v_ref, valid in (
        (wide_own, vo_ref, True),
        (wide_near, vn_ref, near_valid),
        (wide_far, vf_ref, far_valid),
    ):
        for c in range(blocks):
            rows = slice(c * ROWS, (c + 1) * ROWS)
            block = jnp.concatenate([v_ref[rows], ones], axis=1)
            if valid is not True:
                block = block * jnp.where(valid, 1.0, 0.0).astype(bf16)
            wide[rows] = block
    causal = lax.broadcasted_iota(jnp.int32, (ROWS, ROWS), 0) >= lax.broadcasted_iota(
        jnp.int32, (ROWS, ROWS), 1
    )

    def raised(q, keys):
        return jnp.exp2(dot(q, keys, ((1,), (1,))) * power).astype(bf16)

    wrong = jnp.zeros((ROWS, HD), f32)
    for b in range(blocks):
        rows = slice(b * ROWS, (b + 1) * ROWS)
        q = q_ref[rows]
        own = dot(q, ko_ref[rows], ((1,), (1,)))
        far = dot(q, kf_ref[rows], ((1,), (1,)))
        edge = jnp.exp2(jnp.where(causal, own, far) * power)
        total = dot(jnp.where(causal, edge, 0.0).astype(bf16), wide_own[rows])
        total += dot(jnp.where(causal, 0.0, edge).astype(bf16), wide_far[rows])
        total += dot(raised(q, kn_ref[...]), wide_near[...])
        if b > 0:
            total += dot(raised(q, ko_ref[: b * ROWS]), wide_own[: b * ROWS])
        if b < blocks - 1:
            total += dot(raised(q, kf_ref[(b + 1) * ROWS :]), wide_far[(b + 1) * ROWS :])
        sums = total[:, HD:]
        attended_ref[rows] = total[:, :HD] / sums
        fine = (sums > LEAST_SUM) & (sums < MOST_SUM)
        wrong = jnp.maximum(wrong, jnp.where(fine, 0.0, 1.0))

    @pl.when(jnp.max(wrong) > 0.0)
    def _():
        def one_block(b, carry):
            rows = pl.ds(pl.multiple_of(b * ROWS, ROWS), ROWS)
            q = q_ref[rows]
            place = b * ROWS + lax.broadcasted_iota(jnp.int32, (ROWS, tokens), 0)
            column = lax.broadcasted_iota(jnp.int32, (ROWS, tokens), 1)
            limit = jnp.where(far_valid, tokens, -1)
            least = jnp.where(near_valid, 0, tokens)
            lowest = jnp.float32(-jnp.inf)
            far = dot(q, kf_ref[...], ((1,), (1,))) * scale
            far = jnp.where((column > place) & (column < limit), far, lowest)
            near = dot(q, kn_ref[...], ((1,), (1,))) * scale
            near = jnp.where(column >= least, near, lowest)
            own = dot(q, ko_ref[...], ((1,), (1,))) * scale
            own = jnp.where(column <= place, own, lowest)
            most = jnp.maximum(
                jnp.maximum(
                    jnp.max(far, axis=1, keepdims=True), jnp.max(near, axis=1, keepdims=True)
                ),
                jnp.max(own, axis=1, keepdims=True),
            )
            total = jnp.zeros((ROWS, HD), f32)
            sums = jnp.zeros((ROWS, 1), f32)
            for scores, v_ref in ((far, vf_ref), (near, vn_ref), (own, vo_ref)):
                e = jnp.exp(scores - most)
                sums += jnp.sum(e, axis=1, keepdims=True)
                total += dot(e.astype(bf16), v_ref[...])
            attended_ref[rows] = total / sums
            return carry

        lax.fori_loop(0, blocks, one_block, 0)

    low_gate = wg_ref[0].astype(bf16)
    low_up = wu_ref[0].astype(bf16)
    low_down = wd_ref[0].astype(bf16)
    for b in range(blocks):
        rows = slice(b * ROWS, (b + 1) * ROWS)
        q = q_ref[rows]
        gate_pre = dot(q, low_gate)
        hidden = (gate_pre * sigmoid(gate_pre) * dot(q, low_up)).astype(bf16)
        applied = dot(hidden, low_down, ((1,), (1,)))
        mean = jnp.mean(applied * applied, axis=1, keepdims=True)
        normed = applied * lax.rsqrt(mean + rms_epsilon) * gain_ref[...]
        out_ref[rows] = (normed + attended_ref[rows]).astype(bf16)


def mix(first_group, rank, queries, own, near, far, weights, gain):
    tokens, width = queries.shape
    heads = width // HD
    head = pl.BlockSpec((tokens, HD), lambda h: (0, h))
    weight = pl.BlockSpec((1, HD, FW), lambda h: (h, 0, 0))
    return pl.pallas_call(
        functools.partial(mix_kernel, first_group),
        out_shape=jax.ShapeDtypeStruct((tokens, width), bf16),
        grid=(heads,),
        in_specs=[pl.BlockSpec(memory_space=pltpu.SMEM)]
        + [head] * 7
        + [weight] * 3
        + [pl.BlockSpec((1, HD), lambda h: (0, h))],
        out_specs=head,
        scratch_shapes=[pltpu.VMEM((tokens, 2 * HD), bf16)] * 3 + [pltpu.VMEM((tokens, HD), f32)],
        compiler_params=pltpu.CompilerParams(vmem_limit_bytes=VMEM_LIMIT),
        cost_estimate=pl.CostEstimate(
            flops=heads * tokens * 2 * tokens * 8 * HD,
            bytes_accessed=16 * tokens * width,
            transcendentals=heads * tokens * 2 * tokens,
        ),
        name="mix",
    )(rank, queries, *own, *near, *far, *weights, gain)


def sum_over_seq(partial):
    size = lax.axis_size("seq")
    tiles = partial.reshape(size, -1, HD)
    arrived = lax.all_to_all(tiles, "seq", 0, 0, tiled=True)
    part = jnp.sum(arrived.astype(f32), axis=0).astype(bf16)
    copies = jnp.broadcast_to(part, tiles.shape)
    return lax.all_to_all(copies, "seq", 0, 0, tiled=True).reshape(partial.shape)


def body(
    query_vectors,
    key_vectors,
    value_vectors,
    token_rates,
    gate_weight,
    up_weight,
    down_weight,
    step_sizes,
    norm_gain,
):
    rank = lax.axis_index("seq")
    size = lax.axis_size("seq")
    first = (gate_weight, up_weight, down_weight)
    gain = norm_gain.reshape(1, -1)
    ranks = rank.astype(jnp.int32).reshape(1)
    groups = query_vectors.shape[0]
    own = [(key_vectors[g], value_vectors[g]) for g in range(groups)]
    context = []
    for g in range(groups):
        sent = own[g]
        if g > 0:
            sent = tuple(jnp.where(rank >= size - 2, a, b) for a, b in zip(own[g - 1], own[g]))
        far = tuple(move(a, lambda i: (i + 2) % size) for a in sent)
        near = tuple(
            move(jnp.where(rank % 2 == 0, a, b), lambda i: i ^ 1) for a, b in zip(own[g], far)
        )
        context.append((near, far))
    weights = first
    mixed = []
    for g in range(groups):
        partial = local_grads(*own[g], token_rates[g], weights)
        summed = sum_over_seq(partial)
        mixed.append(mix(g == 0, ranks, query_vectors[g], own[g], *context[g], weights, gain))
        weights = step(summed, weights, first, step_sizes)
    return jnp.stack(mixed), jnp.stack(weights)


def solution(mesh):
    return jax.shard_map(
        body,
        mesh=mesh,
        in_specs=(
            P("batch", "seq", "head"),
            P("batch", "seq", "head"),
            P("batch", "seq", "head"),
            P("batch", "head", "seq"),
            P("head", None, None),
            P("head", None, None),
            P("head", None, None),
            P("head"),
            P("head"),
        ),
        out_specs=(P("batch", "seq", "head"), P("batch", "head", None, None)),
        check_vma=False,
    )
```

```python
import functools
import math

import jax
import jax.numpy as jnp
from jax import lax
from jax.experimental import pallas as pl
from jax.experimental.pallas import tpu as pltpu
from jax.sharding import PartitionSpec as P

HD = 128
FW = 256
NS_STEPS = 5
ROWS = 256

coeff_first = 3.4445
coeff_second = -4.775
coeff_third = 2.0315
frob_epsilon = 1e-07
rms_epsilon = 1e-06
column_epsilon = 1e-06

f32 = jnp.float32
bf16 = jnp.bfloat16
LEAST_SUM = 1e-25
MOST_SUM = 1e30
VMEM_LIMIT = 62 * 1024 * 1024
SMALL_LIMIT = 24 * 1024 * 1024
STEP_LIMIT = 24 * 1024 * 1024


def dot(a, b, over=((1,), (0,))):
    return lax.dot_general(a, b, (over, ((), ())), preferred_element_type=f32)


def sigmoid(x):
    return 0.5 * jnp.tanh(0.5 * x) + 0.5


def move(block, route):
    return lax.ppermute(block, "seq", [(i, route(i)) for i in range(lax.axis_size("seq"))])


def fetch(copies, sems, at=0):
    started = [pltpu.make_async_copy(a, b, sems.at[at + i]) for i, (a, b) in enumerate(copies)]
    for copy in started:
        copy.start()
    return started


def fetch(copies, sems, at=0):
    started = [pltpu.make_async_copy(a, b, sems.at[at + i]) for i, (a, b) in enumerate(copies)]
    for copy in started:
        copy.start()
    return started


def grads_kernel(k_ref, v_ref, r_ref, *refs):
    *w_refs, out_ref, grad_ref, hid_ref, og_ref = refs
    if len(w_refs) > 1:
        step_ref, *w_refs, kept_ref, limits_ref = w_refs
        for which in range(3):
            weight = w_refs[which][...]
            kept_ref[which] = weight
            limits_ref[which, :, :1] = jnp.sqrt(jnp.sum(weight * weight, axis=1, keepdims=True))
            for h in range(weight.shape[0]):
                limits_ref[which, h, 1:] = jnp.full((1, FW), step_ref[h], f32)
    else:
        w_refs = [w_refs[0].at[which] for which in range(3)]
    tokens, width = k_ref.shape
    for h in range(width // HD):
        lanes = slice(h * HD, (h + 1) * HD)
        low_gate, low_up, low_down = (w_ref[h].astype(bf16) for w_ref in w_refs)
        for c in range(tokens // ROWS):
            rows = slice(c * ROWS, (c + 1) * ROWS)
            keys = k_ref[rows, lanes]
            rate = jnp.broadcast_to(r_ref[h : h + 1, rows], (HD, ROWS)).T
            out_grad = (-rate * v_ref[rows, lanes].astype(f32)).astype(bf16)
            gate_pre = dot(keys, low_gate)
            up_pre = dot(keys, low_up)
            hidden_grad = dot(out_grad, low_down)
            sig = sigmoid(gate_pre)
            active = gate_pre * sig
            og_ref[rows] = out_grad
            hid_ref[rows] = (active * up_pre).astype(bf16)
            grad_ref[rows, FW:] = (hidden_grad * active).astype(bf16)
            grad_ref[rows, :FW] = (
                hidden_grad * up_pre * sig * (1.0 + gate_pre * (1.0 - sig))
            ).astype(bf16)
        both = dot(k_ref[:, lanes], grad_ref[...], ((0,), (0,)))
        down = dot(og_ref[...], hid_ref[...], ((0,), (0,)))
        for which, full in enumerate((both[:, :FW], both[:, FW:], down)):
            for half in range(2):
                out_ref[which, h, half] = full[:, half * HD : (half + 1) * HD].astype(bf16)


def local_grads(group, keys, values, rates, weights, step_sizes=None):
    _, tokens, width = keys.shape
    heads = width // HD
    extra = [] if step_sizes is None else [step_sizes]
    group_rows = pl.BlockSpec((None, tokens, width), lambda i: (group, 0, 0))
    whole = [pl.BlockSpec(w.shape, lambda i, n=w.ndim: (0,) * n) for w in weights]
    out_shape = [jax.ShapeDtypeStruct((3, heads, 2, HD, HD), bf16)]
    if extra:
        out_shape = [
            jax.ShapeDtypeStruct((3, heads, HD, FW), f32),
            jax.ShapeDtypeStruct((3, heads, 2, FW), f32),
        ] + out_shape
    return pl.pallas_call(
        grads_kernel,
        out_shape=out_shape,
        grid=(1,),
        in_specs=[group_rows] * 2
        + [pl.BlockSpec((None, heads, tokens), lambda i: (group, 0, 0))]
        + [pl.BlockSpec(memory_space=pltpu.SMEM)] * len(extra)
        + whole,
        out_specs=[pl.BlockSpec(o.shape, lambda i, n=len(o.shape): (0,) * n) for o in out_shape],
        scratch_shapes=[
            pltpu.VMEM((tokens, 2 * FW), bf16),
            pltpu.VMEM((tokens, FW), bf16),
            pltpu.VMEM((tokens, HD), bf16),
        ],
        compiler_params=pltpu.CompilerParams(vmem_limit_bytes=VMEM_LIMIT),
        cost_estimate=pl.CostEstimate(
            flops=12 * heads * tokens * HD * FW,
            bytes_accessed=4 * tokens * width,
            transcendentals=heads * tokens * FW,
        ),
        name="local_grads",
    )(keys, values, rates, *extra, *weights)


def split(x):
    high = x.astype(bf16)
    return high, (x - high.astype(f32)).astype(bf16)


def sweeps(x_ref, count):
    def sweep(_, carry):
        pieces, grams, polynomials = [], [], []
        for m in range(count):
            high, low = split(x_ref[m])
            pieces.append((high, low))
            stacked = jnp.concatenate([high, low], axis=0)
            g = dot(stacked, stacked, ((1,), (1,)))
            grams.append(g[:HD, :HD] + (g[HD:, :HD] + g[:HD, HD:]) + g[HD:, HD:])
        for m in range(count):
            row = jnp.concatenate(split(grams[m]), axis=1)
            squared = dot(row, jnp.concatenate([row, row], axis=0))
            polynomials.append(
                coeff_second * grams[m] + coeff_third * (squared[:, :HD] + squared[:, HD:])
            )
        for m in range(count):
            high, low = pieces[m]
            row = jnp.concatenate(split(polynomials[m]), axis=1)
            product = dot(row, jnp.concatenate([high, high], axis=0)) + dot(
                row, jnp.concatenate([low, low], axis=0)
            )
            x_ref[m] = coeff_first * x_ref[m] + product
        return carry

    lax.fori_loop(0, NS_STEPS, sweep, 0)


def step_kernel(s_ref, w_hbm, limits_hbm, out_hbm, x_ref, w_ref, limits_ref, out_ref, sems):
    heads = out_ref.shape[1]
    started = fetch([(w_hbm, w_ref), (limits_hbm, limits_ref)], sems)
    for which in range(3):
        for h in range(heads):
            grad = jnp.concatenate([s_ref[which, h, 0], s_ref[which, h, 1]], axis=1).astype(f32)
            frobenius = jnp.sqrt(jnp.sum(grad * grad, keepdims=True))
            x_ref[which * heads + h] = grad / (frobenius + frob_epsilon)
    sweeps(x_ref, 3 * heads)
    for copy in started:
        copy.wait()
    written = []
    for which in range(3):
        for h in range(heads):
            target = limits_ref[which, h, :1]
            stepped = w_ref[which, h] - limits_ref[which, h, 1:] * x_ref[which * heads + h]
            length = jnp.sqrt(jnp.sum(stepped * stepped, axis=0, keepdims=True))
            out_ref[which, h] = stepped * (target / (length + column_epsilon))
        copy = pltpu.make_async_copy(out_ref.at[which], out_hbm.at[which], sems.at[2 + which])
        copy.start()
        written.append(copy)
    for copy in written:
        copy.wait()


def step(summed, weights, limits):
    heads = weights.shape[1]
    everywhere = pl.BlockSpec(memory_space=pl.ANY)
    return pl.pallas_call(
        step_kernel,
        out_shape=jax.ShapeDtypeStruct(weights.shape, f32),
        in_specs=[pl.BlockSpec(memory_space=pltpu.VMEM), everywhere, everywhere],
        out_specs=everywhere,
        scratch_shapes=[
            pltpu.VMEM((3 * heads, HD, FW), f32),
            pltpu.VMEM(weights.shape, f32),
            pltpu.VMEM(limits.shape, f32),
            pltpu.VMEM(weights.shape, f32),
            pltpu.SemaphoreType.DMA((5,)),
        ],
        compiler_params=pltpu.CompilerParams(vmem_limit_bytes=STEP_LIMIT),
        cost_estimate=pl.CostEstimate(
            flops=3 * heads * NS_STEPS * 40 * HD * HD * FW,
            bytes_accessed=3 * heads * 10 * HD * FW,
            transcendentals=0,
        ),
        name="weight_step",
    )(summed, weights, limits)


def mix_kernel(group, rank_ref, *refs):
    (
        q_hbm, k_hbm, v_hbm, ks_hbm, vs_hbm, kf_hbm, vf_hbm, kb_hbm, vb_hbm, w_hbm, gain_hbm,
        out_hbm, q_ref, ko_ref, vo_ref, kf_ref, vf_ref, kn_ref, vn_ref, w_ref, gain_ref,
        normed_ref, out_ref, sems,
    ) = refs
    tokens, width = q_ref.shape
    heads = width // HD
    scale = 1.0 / math.sqrt(HD)
    power = scale * math.log2(math.e)
    blocks = tokens // ROWS
    odd = rank_ref[0] % 2 == 1
    started = fetch(
        [
            (w_hbm, w_ref),
            (gain_hbm, gain_ref),
            (q_hbm.at[group], q_ref),
            (k_hbm.at[group], ko_ref),
            (v_hbm.at[group], vo_ref),
            (kf_hbm, kf_ref),
            (vf_hbm, vf_ref),
        ],
        sems,
    )
    beside = [(ks_hbm.at[group], kn_ref), (vs_hbm.at[group], vn_ref)]
    behind = [(kb_hbm, kn_ref), (vb_hbm, vn_ref)]

    @pl.when(odd)
    def _():
        fetch(beside, sems, 7)

    @pl.when(jnp.logical_not(odd))
    def _():
        fetch(behind, sems, 7)

    started += [pltpu.make_async_copy(a, b, sems.at[7 + i]) for i, (a, b) in enumerate(behind)]
    for copy in started[:3]:
        copy.wait()
    all_lanes = [slice(h * HD, (h + 1) * HD) for h in range(heads)]
    all_rows = [slice(b * ROWS, (b + 1) * ROWS) for b in range(blocks)]
    for h, lanes in enumerate(all_lanes):
        low_gate, low_up, low_down = (w_ref[which, h].astype(bf16) for which in range(3))
        for rows in all_rows:
            q = q_ref[rows, lanes]
            gate_pre = dot(q, low_gate)
            hidden = (gate_pre * sigmoid(gate_pre) * dot(q, low_up)).astype(bf16)
            applied = dot(hidden, low_down, ((1,), (1,)))
            mean = jnp.mean(applied * applied, axis=1, keepdims=True)
            normed_ref[rows, lanes] = applied * lax.rsqrt(mean + rms_epsilon) * gain_ref[:, lanes]
    for copy in started[3:]:
        copy.wait()

    near_valid = rank_ref[0] >= 1 if group == 0 else True
    far_valid = rank_ref[0] >= 2 if group == 0 else True

    def beside_ones(v, valid=True):
        wide = jnp.concatenate([v, jnp.ones((v.shape[0], HD), bf16)], axis=1)
        return wide if valid is True else wide * jnp.where(valid, 1.0, 0.0).astype(bf16)

    causal = lax.broadcasted_iota(jnp.int32, (ROWS, ROWS), 0) >= lax.broadcasted_iota(
        jnp.int32, (ROWS, ROWS), 1
    )

    def raised(q, keys):
        return jnp.exp2(dot(q, keys, ((1,), (1,))) * power).astype(bf16)

    wrong = jnp.zeros((ROWS, HD), f32)
    for lanes in all_lanes:
        for b, rows in enumerate(all_rows):
            q = q_ref[rows, lanes]
            own = dot(q, ko_ref[rows, lanes], ((1,), (1,)))
            far = dot(q, kf_ref[rows, lanes], ((1,), (1,)))
            edge = jnp.exp2(jnp.where(causal, own, far) * power)
            total = dot(
                jnp.where(causal, edge, 0.0).astype(bf16), beside_ones(vo_ref[rows, lanes])
            )
            total += dot(
                jnp.where(causal, 0.0, edge).astype(bf16),
                beside_ones(vf_ref[rows, lanes], far_valid),
            )
            total += dot(raised(q, kn_ref[:, lanes]), beside_ones(vn_ref[:, lanes], near_valid))
            if b > 0:
                past = slice(0, b * ROWS)
                total += dot(raised(q, ko_ref[past, lanes]), beside_ones(vo_ref[past, lanes]))
            if b < blocks - 1:
                rest = slice((b + 1) * ROWS, tokens)
                total += dot(
                    raised(q, kf_ref[rest, lanes]), beside_ones(vf_ref[rest, lanes], far_valid)
                )
            sums = total[:, HD:]
            out_ref[rows, lanes] = (normed_ref[rows, lanes] + total[:, :HD] / sums).astype(bf16)
            fine = (sums > LEAST_SUM) & (sums < MOST_SUM)
            wrong = jnp.maximum(wrong, jnp.where(fine, 0.0, 1.0))

    @pl.when(jnp.max(wrong) > 0.0)
    def _():
        def one_block(b, carry):
            rows = pl.ds(pl.multiple_of(b * ROWS, ROWS), ROWS)
            place = b * ROWS + lax.broadcasted_iota(jnp.int32, (ROWS, tokens), 0)
            column = lax.broadcasted_iota(jnp.int32, (ROWS, tokens), 1)
            limit = jnp.where(far_valid, tokens, -1)
            least = jnp.where(near_valid, 0, tokens)
            lowest = jnp.float32(-jnp.inf)
            for lanes in all_lanes:
                q = q_ref[rows, lanes]
                far = dot(q, kf_ref[:, lanes], ((1,), (1,))) * scale
                far = jnp.where((column > place) & (column < limit), far, lowest)
                near = dot(q, kn_ref[:, lanes], ((1,), (1,))) * scale
                near = jnp.where(column >= least, near, lowest)
                own = dot(q, ko_ref[:, lanes], ((1,), (1,))) * scale
                own = jnp.where(column <= place, own, lowest)
                parts = ((far, vf_ref), (near, vn_ref), (own, vo_ref))
                most = jnp.max(own, axis=1, keepdims=True)
                for scores, _ in parts[:2]:
                    most = jnp.maximum(most, jnp.max(scores, axis=1, keepdims=True))
                total = jnp.zeros((ROWS, HD), f32)
                sums = jnp.zeros((ROWS, 1), f32)
                for scores, v_ref in parts:
                    e = jnp.exp(scores - most)
                    sums += jnp.sum(e, axis=1, keepdims=True)
                    total += dot(e.astype(bf16), v_ref[:, lanes])
                out_ref[rows, lanes] = (normed_ref[rows, lanes] + total / sums).astype(bf16)
            return carry

        lax.fori_loop(0, blocks, one_block, 0)

    done = pltpu.make_async_copy(out_ref, out_hbm.at[group], sems.at[9])
    done.start()
    done.wait()


def mix(group, so_far, rank, queries, keys, values, early, context, weights, gain):
    groups, tokens, width = queries.shape
    heads = width // HD
    earlier = [] if so_far is None else [so_far]
    kernel = functools.partial(mix_kernel, group)
    if earlier:
        kernel = functools.partial(after_earlier, kernel)
    everywhere = pl.BlockSpec(memory_space=pl.ANY)
    block = pltpu.VMEM((tokens, width), bf16)
    return pl.pallas_call(
        kernel,
        out_shape=jax.ShapeDtypeStruct(queries.shape, bf16),
        in_specs=[everywhere] * len(earlier)
        + [pl.BlockSpec(memory_space=pltpu.SMEM)]
        + [everywhere] * 11,
        out_specs=everywhere,
        input_output_aliases={0: 0} if earlier else {},
        scratch_shapes=[block] * 7
        + [
            pltpu.VMEM(weights.shape, f32),
            pltpu.VMEM(gain.shape, f32),
            pltpu.VMEM((tokens, width), f32),
            block,
            pltpu.SemaphoreType.DMA((10,)),
        ],
        compiler_params=pltpu.CompilerParams(vmem_limit_bytes=VMEM_LIMIT),
        cost_estimate=pl.CostEstimate(
            flops=heads * tokens * 2 * tokens * 8 * HD,
            bytes_accessed=16 * tokens * width,
            transcendentals=heads * tokens * 2 * tokens,
        ),
        name="mix",
    )(*earlier, rank, queries, keys, values, *early, *context, weights, gain)


def after_earlier(kernel, _, *refs):
    kernel(*refs)


def add_kernel(x_ref, out_ref):
    total = jnp.sum(x_ref[...].astype(f32), axis=0).astype(bf16)
    for i in range(out_ref.shape[0]):
        out_ref[i] = total


def after(x, event):
    return lax.optimization_barrier((x, event))[0]


def exchange(tiles):
    return lax.all_to_all(tiles, "seq", 0, 0, tiled=True)


def add_parts(arrived):
    vmem = pl.BlockSpec(memory_space=pltpu.VMEM)
    return pl.pallas_call(
        add_kernel,
        out_shape=jax.ShapeDtypeStruct(arrived.shape, bf16),
        in_specs=[vmem],
        out_specs=vmem,
        compiler_params=pltpu.CompilerParams(vmem_limit_bytes=SMALL_LIMIT),
        name="add_parts",
    )(arrived)


def body(
    query_vectors,
    key_vectors,
    value_vectors,
    token_rates,
    gate_weight,
    up_weight,
    down_weight,
    step_sizes,
    norm_gain,
):
    rank = lax.axis_index("seq")
    size = lax.axis_size("seq")
    gain = norm_gain.reshape(1, -1)
    ranks = rank.astype(jnp.int32).reshape(1)

    def block_of(tensor, group):
        own = tensor[group]
        if group > 0:
            own = jnp.where(rank >= size - 2, tensor[group - 1], own)
        return own

    def send_far(block):
        return move(block, lambda i: (i + 2) % size)

    def swap(block):
        return move(block, lambda i: i ^ 1)

    def mix_group(group, so_far, early, context, weights):
        own = (query_vectors, key_vectors, value_vectors)
        return mix(group, so_far, ranks, *own, early, context, weights, gain)

    together = lax.optimization_barrier
    first = (gate_weight, up_weight, down_weight)
    blocks = [[block_of(t, g) for t in (key_vectors, value_vectors)] for g in range(2)]
    far_keys = send_far(blocks[0][0])
    weights, limits, partial = local_grads(
        0, key_vectors, value_vectors, token_rates, first, step_sizes
    )
    far_values = send_far(after(blocks[0][1], (far_keys, partial)))
    added = add_parts(exchange(partial.reshape(size, -1, HD)))
    summed = exchange(added)
    early = [swap(key_vectors), swap(value_vectors)]
    context = (far_keys, far_values, swap(far_keys), swap(far_values))
    far_keys = send_far(after(blocks[1][0], (far_values, summed)))
    later = step(summed.reshape(partial.shape), weights, limits)
    (partial,) = local_grads(1, key_vectors, value_vectors, token_rates, (later,))
    far_values = send_far(after(blocks[1][1], (far_keys, partial)))
    arrived = exchange(partial.reshape(size, -1, HD))
    mixed = mix_group(0, None, early, context, weights)
    arrived, mixed, far_keys, far_values = together((arrived, mixed, far_keys, far_values))
    summed = exchange(add_parts(arrived))
    context = (far_keys, far_values, swap(far_keys), swap(far_values))
    mixed = mix_group(1, mixed, early, context, later)
    summed, mixed = together((summed, mixed))
    last = step(summed.reshape(partial.shape), later, limits)
    return mixed, last


def solution(mesh):
    return jax.shard_map(
        body,
        mesh=mesh,
        in_specs=(
            P("batch", "seq", "head"),
            P("batch", "seq", "head"),
            P("batch", "seq", "head"),
            P("batch", "head", "seq"),
            P("head", None, None),
            P("head", None, None),
            P("head", None, None),
            P("head"),
            P("head"),
        ),
        out_specs=(P("batch", "seq", "head"), P("batch", "head", None, None)),
        check_vma=False,
    )
```

```python
import functools
import math

import jax
import jax.numpy as jnp
from jax import lax
from jax.experimental import pallas as pl
from jax.experimental.pallas import tpu as pltpu
from jax.sharding import PartitionSpec as P

HD = 128
FW = 256
NS_STEPS = 5
ROWS = 256

coeff_first = 3.4445
coeff_second = -4.775
coeff_third = 2.0315
frob_epsilon = 1e-07
rms_epsilon = 1e-06
column_epsilon = 1e-06

f32 = jnp.float32
bf16 = jnp.bfloat16
LEAST_SUM = 1e-25
MOST_SUM = 1e30
NO_KEYS = -1e30
VMEM_LIMIT = 62 * 1024 * 1024
SMALL_LIMIT = 24 * 1024 * 1024
STEP_LIMIT = 24 * 1024 * 1024


def dot(a, b, over=((1,), (0,))):
    return lax.dot_general(a, b, (over, ((), ())), preferred_element_type=f32)


def sigmoid(x):
    return 0.5 * jnp.tanh(0.5 * x) + 0.5


def move(block, route):
    return lax.ppermute(block, "seq", [(i, route(i)) for i in range(lax.axis_size("seq"))])


def fetch(copies, sems, at=0):
    started = [pltpu.make_async_copy(a, b, sems.at[at + i]) for i, (a, b) in enumerate(copies)]
    for copy in started:
        copy.start()
    return started


def fetch(copies, sems, at=0):
    started = [pltpu.make_async_copy(a, b, sems.at[at + i]) for i, (a, b) in enumerate(copies)]
    for copy in started:
        copy.start()
    return started


def grads_kernel(group, k_ref, v_ref, r_ref, *refs):
    if k_ref.ndim == 3:
        k_ref, v_ref, r_ref = k_ref.at[group], v_ref.at[group], r_ref.at[group]
    *w_refs, out_ref, grad_ref, hid_ref, og_ref = refs
    if len(w_refs) > 1:
        step_ref, *w_refs, kept_ref, limits_ref = w_refs
        for which in range(3):
            weight = w_refs[which][...]
            kept_ref[which] = weight
            limits_ref[which, :, :1] = jnp.sqrt(jnp.sum(weight * weight, axis=1, keepdims=True))
            for h in range(weight.shape[0]):
                limits_ref[which, h, 1:] = jnp.full((1, FW), step_ref[h], f32)
    else:
        w_refs = [w_refs[0].at[which] for which in range(3)]
    tokens, width = k_ref.shape
    for h in range(width // HD):
        lanes = slice(h * HD, (h + 1) * HD)
        low_gate, low_up, low_down = (w_ref[h].astype(bf16) for w_ref in w_refs)
        for c in range(tokens // ROWS):
            rows = slice(c * ROWS, (c + 1) * ROWS)
            keys = k_ref[rows, lanes]
            rate = jnp.broadcast_to(r_ref[h : h + 1, rows], (HD, ROWS)).T
            out_grad = (-rate * v_ref[rows, lanes].astype(f32)).astype(bf16)
            gate_pre = dot(keys, low_gate)
            up_pre = dot(keys, low_up)
            hidden_grad = dot(out_grad, low_down)
            sig = sigmoid(gate_pre)
            active = gate_pre * sig
            og_ref[rows] = out_grad
            hid_ref[rows] = (active * up_pre).astype(bf16)
            grad_ref[rows, FW:] = (hidden_grad * active).astype(bf16)
            grad_ref[rows, :FW] = (
                hidden_grad * up_pre * sig * (1.0 + gate_pre * (1.0 - sig))
            ).astype(bf16)
        both = dot(k_ref[:, lanes], grad_ref[...], ((0,), (0,)))
        down = dot(og_ref[...], hid_ref[...], ((0,), (0,)))
        for which, full in enumerate((both[:, :FW], both[:, FW:], down)):
            for half in range(2):
                out_ref[which, h, half] = full[:, half * HD : (half + 1) * HD].astype(bf16)


def local_grads(group, keys, values, rates, weights, step_sizes=None):
    _, tokens, width = keys.shape
    heads = width // HD
    vmem = pl.BlockSpec(memory_space=pltpu.VMEM)
    out_shape = [jax.ShapeDtypeStruct((3, heads, 2, HD, HD), bf16)]
    if step_sizes is None:
        extra, limit = [], SMALL_LIMIT
        in_specs = [vmem] * (3 + len(weights))
        out_specs = [vmem]
    else:
        extra, limit = [step_sizes], VMEM_LIMIT
        group_rows = pl.BlockSpec((None, tokens, width), lambda i: (group, 0, 0))
        in_specs = (
            [group_rows] * 2
            + [pl.BlockSpec((None, heads, tokens), lambda i: (group, 0, 0))]
            + [pl.BlockSpec(memory_space=pltpu.SMEM)]
            + [pl.BlockSpec((heads, HD, FW), lambda i: (0, 0, 0))] * len(weights)
        )
        out_shape = [
            jax.ShapeDtypeStruct((3, heads, HD, FW), f32),
            jax.ShapeDtypeStruct((3, heads, 2, FW), f32),
        ] + out_shape
        out_specs = [pl.BlockSpec(o.shape, lambda i, n=len(o.shape): (0,) * n) for o in out_shape]
    return pl.pallas_call(
        functools.partial(grads_kernel, group),
        out_shape=out_shape,
        grid=(1,) if extra else (),
        in_specs=in_specs,
        out_specs=out_specs,
        scratch_shapes=[
            pltpu.VMEM((tokens, 2 * FW), bf16),
            pltpu.VMEM((tokens, FW), bf16),
            pltpu.VMEM((tokens, HD), bf16),
        ],
        compiler_params=pltpu.CompilerParams(vmem_limit_bytes=limit),
        cost_estimate=pl.CostEstimate(
            flops=12 * heads * tokens * HD * FW,
            bytes_accessed=4 * tokens * width,
            transcendentals=heads * tokens * FW,
        ),
        name="local_grads",
    )(keys, values, rates, *extra, *weights)


def split(x):
    high = x.astype(bf16)
    return high, (x - high.astype(f32)).astype(bf16)


def sweeps(x_ref, count):
    def sweep(_, carry):
        pieces, grams, polynomials = [], [], []
        for m in range(count):
            high, low = split(x_ref[m])
            pieces.append((high, low))
            stacked = jnp.concatenate([high, low], axis=0)
            g = dot(stacked, stacked, ((1,), (1,)))
            grams.append(g[:HD, :HD] + (g[HD:, :HD] + g[:HD, HD:]) + g[HD:, HD:])
        for m in range(count):
            row = jnp.concatenate(split(grams[m]), axis=1)
            squared = dot(row, jnp.concatenate([row, row], axis=0))
            polynomials.append(
                coeff_second * grams[m] + coeff_third * (squared[:, :HD] + squared[:, HD:])
            )
        for m in range(count):
            high, low = pieces[m]
            row = jnp.concatenate(split(polynomials[m]), axis=1)
            product = dot(row, jnp.concatenate([high, high], axis=0)) + dot(
                row, jnp.concatenate([low, low], axis=0)
            )
            x_ref[m] = coeff_first * x_ref[m] + product
        return carry

    lax.fori_loop(0, NS_STEPS, sweep, 0)


def step_kernel(s_ref, w_hbm, limits_hbm, out_hbm, x_ref, w_ref, limits_ref, out_ref, sems):
    heads = out_ref.shape[1]
    started = fetch([(w_hbm, w_ref), (limits_hbm, limits_ref)], sems)
    for which in range(3):
        for h in range(heads):
            grad = jnp.concatenate([s_ref[which, h, 0], s_ref[which, h, 1]], axis=1).astype(f32)
            frobenius = jnp.sqrt(jnp.sum(grad * grad, keepdims=True))
            x_ref[which * heads + h] = grad / (frobenius + frob_epsilon)
    sweeps(x_ref, 3 * heads)
    for copy in started:
        copy.wait()
    written = []
    for which in range(3):
        for h in range(heads):
            target = limits_ref[which, h, :1]
            stepped = w_ref[which, h] - limits_ref[which, h, 1:] * x_ref[which * heads + h]
            length = jnp.sqrt(jnp.sum(stepped * stepped, axis=0, keepdims=True))
            out_ref[which, h] = stepped * (target / (length + column_epsilon))
        copy = pltpu.make_async_copy(out_ref.at[which], out_hbm.at[which], sems.at[2 + which])
        copy.start()
        written.append(copy)
    for copy in written:
        copy.wait()


def step(summed, weights, limits):
    heads = weights.shape[1]
    everywhere = pl.BlockSpec(memory_space=pl.ANY)
    return pl.pallas_call(
        step_kernel,
        out_shape=jax.ShapeDtypeStruct(weights.shape, f32),
        in_specs=[pl.BlockSpec(memory_space=pltpu.VMEM), everywhere, everywhere],
        out_specs=everywhere,
        scratch_shapes=[
            pltpu.VMEM((3 * heads, HD, FW), f32),
            pltpu.VMEM(weights.shape, f32),
            pltpu.VMEM(limits.shape, f32),
            pltpu.VMEM(weights.shape, f32),
            pltpu.SemaphoreType.DMA((5,)),
        ],
        compiler_params=pltpu.CompilerParams(vmem_limit_bytes=STEP_LIMIT),
        cost_estimate=pl.CostEstimate(
            flops=3 * heads * NS_STEPS * 40 * HD * HD * FW,
            bytes_accessed=3 * heads * 10 * HD * FW,
            transcendentals=0,
        ),
        name="weight_step",
    )(summed, weights, limits)


def mix_kernel(group, rank_ref, *refs):
    (
        q_hbm, k_hbm, v_hbm, ks_hbm, vs_hbm, kf_hbm, vf_hbm, kb_hbm, vb_hbm, w_hbm, gain_hbm,
        out_hbm, q_ref, ko_ref, vo_ref, kf_ref, vf_ref, kn_ref, vn_ref, w_ref, gain_ref,
        normed_ref, out_ref, sems,
    ) = refs
    tokens, width = q_ref.shape
    heads = width // HD
    scale = 1.0 / math.sqrt(HD)
    power = scale * math.log2(math.e)
    blocks = tokens // ROWS
    odd = rank_ref[0] % 2 == 1
    started = fetch(
        [
            (w_hbm, w_ref),
            (gain_hbm, gain_ref),
            (q_hbm.at[group], q_ref),
            (k_hbm.at[group], ko_ref),
            (v_hbm.at[group], vo_ref),
            (kf_hbm, kf_ref),
            (vf_hbm, vf_ref),
        ],
        sems,
    )
    beside = [(ks_hbm.at[group], kn_ref), (vs_hbm.at[group], vn_ref)]
    behind = [(kb_hbm, kn_ref), (vb_hbm, vn_ref)]

    @pl.when(odd)
    def _():
        fetch(beside, sems, 7)

    @pl.when(jnp.logical_not(odd))
    def _():
        fetch(behind, sems, 7)

    started += [pltpu.make_async_copy(a, b, sems.at[7 + i]) for i, (a, b) in enumerate(behind)]
    for copy in started[:3]:
        copy.wait()
    all_lanes = [slice(h * HD, (h + 1) * HD) for h in range(heads)]
    all_rows = [slice(b * ROWS, (b + 1) * ROWS) for b in range(blocks)]
    for h, lanes in enumerate(all_lanes):
        low_gate, low_up, low_down = (w_ref[which, h].astype(bf16) for which in range(3))
        for rows in all_rows:
            q = q_ref[rows, lanes]
            gate_pre = dot(q, low_gate)
            hidden = (gate_pre * sigmoid(gate_pre) * dot(q, low_up)).astype(bf16)
            applied = dot(hidden, low_down, ((1,), (1,)))
            mean = jnp.mean(applied * applied, axis=1, keepdims=True)
            normed_ref[rows, lanes] = applied * lax.rsqrt(mean + rms_epsilon) * gain_ref[:, lanes]
    for copy in started[3:]:
        copy.wait()

    near_valid = rank_ref[0] >= 1 if group == 0 else True
    far_valid = rank_ref[0] >= 2 if group == 0 else True

    def beside_ones(v, valid=True):
        wide = jnp.concatenate([v, jnp.ones((v.shape[0], HD), bf16)], axis=1)
        return wide if valid is True else wide * jnp.where(valid, 1.0, 0.0).astype(bf16)

    causal = lax.broadcasted_iota(jnp.int32, (ROWS, ROWS), 0) >= lax.broadcasted_iota(
        jnp.int32, (ROWS, ROWS), 1
    )

    def raised(q, keys):
        return jnp.exp2(dot(q, keys, ((1,), (1,))) * power).astype(bf16)

    wrong = jnp.zeros((ROWS, HD), f32)
    for lanes in all_lanes:
        for b, rows in enumerate(all_rows):
            q = q_ref[rows, lanes]
            own = dot(q, ko_ref[rows, lanes], ((1,), (1,)))
            far = dot(q, kf_ref[rows, lanes], ((1,), (1,)))
            edge = jnp.exp2(jnp.where(causal, own, far) * power)
            total = dot(
                jnp.where(causal, edge, 0.0).astype(bf16), beside_ones(vo_ref[rows, lanes])
            )
            total += dot(
                jnp.where(causal, 0.0, edge).astype(bf16),
                beside_ones(vf_ref[rows, lanes], far_valid),
            )
            total += dot(raised(q, kn_ref[:, lanes]), beside_ones(vn_ref[:, lanes], near_valid))
            if b > 0:
                past = slice(0, b * ROWS)
                total += dot(raised(q, ko_ref[past, lanes]), beside_ones(vo_ref[past, lanes]))
            if b < blocks - 1:
                rest = slice((b + 1) * ROWS, tokens)
                total += dot(
                    raised(q, kf_ref[rest, lanes]), beside_ones(vf_ref[rest, lanes], far_valid)
                )
            sums = total[:, HD:]
            out_ref[rows, lanes] = (normed_ref[rows, lanes] + total[:, :HD] / sums).astype(bf16)
            fine = (sums > LEAST_SUM) & (sums < MOST_SUM)
            wrong = jnp.maximum(wrong, jnp.where(fine, 0.0, 1.0))

    @pl.when(jnp.max(wrong) > 0.0)
    def _():
        def one_block(b, carry):
            rows = pl.ds(pl.multiple_of(b * ROWS, ROWS), ROWS)
            place = b * ROWS + lax.broadcasted_iota(jnp.int32, (ROWS, tokens), 0)
            column = lax.broadcasted_iota(jnp.int32, (ROWS, tokens), 1)
            limit = jnp.where(far_valid, tokens, -1)
            least = jnp.where(near_valid, 0, tokens)
            lowest = jnp.float32(-jnp.inf)
            for lanes in all_lanes:
                q = q_ref[rows, lanes]
                far = dot(q, kf_ref[:, lanes], ((1,), (1,))) * scale
                far = jnp.where((column > place) & (column < limit), far, lowest)
                near = dot(q, kn_ref[:, lanes], ((1,), (1,))) * scale
                near = jnp.where(column >= least, near, lowest)
                own = dot(q, ko_ref[:, lanes], ((1,), (1,))) * scale
                own = jnp.where(column <= place, own, lowest)
                parts = ((far, vf_ref), (near, vn_ref), (own, vo_ref))
                most = jnp.max(own, axis=1, keepdims=True)
                for scores, _ in parts[:2]:
                    most = jnp.maximum(most, jnp.max(scores, axis=1, keepdims=True))
                total = jnp.zeros((ROWS, HD), f32)
                sums = jnp.zeros((ROWS, 1), f32)
                for scores, v_ref in parts:
                    e = jnp.exp(scores - most)
                    sums += jnp.sum(e, axis=1, keepdims=True)
                    total += dot(e.astype(bf16), v_ref[:, lanes])
                out_ref[rows, lanes] = (normed_ref[rows, lanes] + total / sums).astype(bf16)
            return carry

        lax.fori_loop(0, blocks, one_block, 0)

    done = pltpu.make_async_copy(out_ref, out_hbm.at[group], sems.at[9])
    done.start()
    done.wait()


def mix(group, rank, queries, keys, values, early, context, weights, gain):
    groups, tokens, width = queries.shape
    heads = width // HD
    everywhere = pl.BlockSpec(memory_space=pl.ANY)
    block = pltpu.VMEM((tokens, width), bf16)
    return pl.pallas_call(
        functools.partial(mix_kernel, group),
        out_shape=jax.ShapeDtypeStruct(queries.shape, bf16),
        in_specs=[pl.BlockSpec(memory_space=pltpu.SMEM)] + [everywhere] * 11,
        out_specs=everywhere,
        scratch_shapes=[block] * 7
        + [
            pltpu.VMEM(weights.shape, f32),
            pltpu.VMEM(gain.shape, f32),
            pltpu.VMEM((tokens, width), f32),
            block,
            pltpu.SemaphoreType.DMA((10,)),
        ],
        compiler_params=pltpu.CompilerParams(vmem_limit_bytes=VMEM_LIMIT),
        cost_estimate=pl.CostEstimate(
            flops=heads * tokens * 2 * tokens * 8 * HD,
            bytes_accessed=16 * tokens * width,
            transcendentals=heads * tokens * 2 * tokens,
        ),
        name="mix",
    )(rank, queries, keys, values, *early, *context, weights, gain)


def raise_to(q, keys):
    power = math.log2(math.e) / math.sqrt(HD)
    return jnp.exp2(dot(q, keys, ((1,), (1,))) * power)


def with_ones(v):
    return jnp.concatenate([v, jnp.ones((v.shape[0], HD), bf16)], axis=1)


def weighted(e, v):
    return dot(e.astype(bf16), with_ones(v))


def from_maximum(q, parts):
    scores = []
    most = jnp.full((q.shape[0], 1), NO_KEYS, f32)
    for keys, _, allowed in parts:
        s = dot(q, keys, ((1,), (1,))) / math.sqrt(HD)
        scores.append(s)
        most = jnp.maximum(
            most, jnp.max(jnp.where(allowed, s, NO_KEYS), axis=1, keepdims=True)
        )
    total = jnp.zeros((q.shape[0], HD), f32)
    sums = jnp.zeros((q.shape[0], 1), f32)
    for s, (_, values, allowed) in zip(scores, parts):
        e = jnp.where(allowed, jnp.exp(jnp.where(allowed, s, most) - most), 0.0)
        sums += jnp.sum(e, axis=1, keepdims=True)
        total += dot(e.astype(bf16), values)
    some = sums > 0.0
    safe = jnp.where(some, sums, 1.0)
    level = jnp.where(some, most + jnp.log(safe), NO_KEYS)
    return total / safe, jnp.broadcast_to(level, total.shape)


def unsafe(sums):
    return jnp.where((sums > LEAST_SUM) & (sums < MOST_SUM), 0.0, 1.0)


def places(first_row, tokens):
    row = first_row + lax.broadcasted_iota(jnp.int32, (ROWS, tokens), 0)
    return row, lax.broadcasted_iota(jnp.int32, (ROWS, tokens), 1)


def part_kernel(group, size, remote, rank_ref, *refs):
    (
        q_hbm, k_hbm, v_hbm, ks_hbm, vs_hbm, out_ref, level_ref,
        q_ref, ko_ref, vo_ref, ks_ref, vs_ref, total_ref, sems,
    ) = refs
    tokens, width = q_ref.shape
    heads = width // HD
    blocks = tokens // ROWS
    rank = rank_ref[0]
    both_shards = rank % 2 == (0 if remote else 1)
    at = jnp.where(rank >= size - 2, group - 1, group) if remote else group
    started = fetch(
        [
            (q_hbm if remote else q_hbm.at[group], q_ref),
            (k_hbm.at[at], ko_ref),
            (v_hbm.at[at], vo_ref),
            (ks_hbm.at[at], ks_ref),
            (vs_hbm.at[at], vs_ref),
        ],
        sems,
    )
    for copy in started[:3]:
        copy.wait()
    all_lanes = [slice(h * HD, (h + 1) * HD) for h in range(heads)]
    all_rows = [slice(b * ROWS, (b + 1) * ROWS) for b in range(blocks)]
    row, column = places(0, ROWS)
    for h, lanes in enumerate(all_lanes):
        for b, rows in enumerate(all_rows):
            q = q_ref[rows, lanes]
            inside = column > row if remote else column <= row
            e = jnp.where(inside, raise_to(q, ko_ref[rows, lanes]), 0.0)
            total = weighted(e, vo_ref[rows, lanes])
            rest = slice((b + 1) * ROWS, tokens) if remote else slice(0, b * ROWS)
            if rest.start < rest.stop:
                total += weighted(raise_to(q, ko_ref[rest, lanes]), vo_ref[rest, lanes])
            total_ref[h, rows] = total
    for copy in started[3:]:
        copy.wait()

    @pl.when(both_shards)
    def _():
        for h, lanes in enumerate(all_lanes):
            for rows in all_rows:
                e = raise_to(q_ref[rows, lanes], ks_ref[:, lanes])
                total_ref[h, rows] += weighted(e, vs_ref[:, lanes])

    wrong = jnp.zeros((ROWS, HD), f32)
    for h, lanes in enumerate(all_lanes):
        for b, rows in enumerate(all_rows):
            total = total_ref[h, rows]
            sums = total[:, HD:]
            some = sums > 0.0
            safe = jnp.where(some, sums, 1.0)
            out_ref[rows, lanes] = (total[:, :HD] / safe).astype(out_ref.dtype)
            level = jnp.where(some, jnp.log(safe), NO_KEYS)
            level_ref[h, :, rows] = level.T[:8]
            bad = unsafe(sums)
            if remote and b == blocks - 1:
                last = lax.broadcasted_iota(jnp.int32, bad.shape, 0) == ROWS - 1
                bad = jnp.where(last & jnp.logical_not(both_shards), 0.0, bad)
            wrong = jnp.maximum(wrong, bad)

    @pl.when(jnp.max(wrong) > 0.0)
    def _():
        def one_block(b, carry):
            rows = pl.ds(pl.multiple_of(b * ROWS, ROWS), ROWS)
            row, column = places(b * ROWS, tokens)
            everyone = column >= jnp.where(both_shards, 0, tokens)
            for h, lanes in enumerate(all_lanes):
                parts = (
                    (ko_ref[:, lanes], vo_ref[:, lanes], column > row if remote else column <= row),
                    (ks_ref[:, lanes], vs_ref[:, lanes], everyone),
                )
                values, level = from_maximum(q_ref[rows, lanes], parts)
                out_ref[rows, lanes] = values.astype(out_ref.dtype)
                level_ref[h, :, rows] = level.T[:8]
            return carry

        lax.fori_loop(0, blocks, one_block, 0)


def part(group, size, remote, rank, queries, keys, values, early):
    _, tokens, width = keys.shape
    heads = width // HD
    everywhere = pl.BlockSpec(memory_space=pl.ANY)
    block = pltpu.VMEM((tokens, width), bf16)
    return pl.pallas_call(
        functools.partial(part_kernel, group, size, remote),
        out_shape=[
            jax.ShapeDtypeStruct((tokens, width), bf16 if remote else f32),
            jax.ShapeDtypeStruct((heads, 8, tokens), f32),
        ],
        in_specs=[pl.BlockSpec(memory_space=pltpu.SMEM)] + [everywhere] * 5,
        out_specs=[pl.BlockSpec()] * 2,
        scratch_shapes=[block] * 5
        + [pltpu.VMEM((heads, tokens, 2 * HD), f32), pltpu.SemaphoreType.DMA((5,))],
        compiler_params=pltpu.CompilerParams(vmem_limit_bytes=VMEM_LIMIT),
        cost_estimate=pl.CostEstimate(
            flops=heads * tokens * tokens * 8 * HD,
            bytes_accessed=12 * tokens * width,
            transcendentals=heads * tokens * tokens,
        ),
        name="remote_part" if remote else "local_part",
    )(rank, queries, keys, values, *early)


def finish_kernel(group, _, *refs):
    (
        q_hbm, near_hbm, near_level_hbm, far_hbm, far_level_hbm, w_hbm, gain_hbm, out_hbm,
        q_ref, near_ref, near_level, far_ref, far_level, w_ref, gain_ref, out_ref, sems,
    ) = refs
    tokens, width = q_ref.shape
    started = fetch(
        [
            (w_hbm, w_ref),
            (gain_hbm, gain_ref),
            (q_hbm.at[group], q_ref),
            (near_hbm, near_ref),
            (near_level_hbm, near_level),
            (far_hbm, far_ref),
            (far_level_hbm, far_level),
        ],
        sems,
    )
    for copy in started:
        copy.wait()
    for h in range(width // HD):
        lanes = slice(h * HD, (h + 1) * HD)
        low_gate, low_up, low_down = (w_ref[which, h].astype(bf16) for which in range(3))
        for b in range(tokens // ROWS):
            rows = slice(b * ROWS, (b + 1) * ROWS)
            q = q_ref[rows, lanes]
            gate_pre = dot(q, low_gate)
            hidden = (gate_pre * sigmoid(gate_pre) * dot(q, low_up)).astype(bf16)
            applied = dot(hidden, low_down, ((1,), (1,)))
            mean = jnp.mean(applied * applied, axis=1, keepdims=True)
            normed = applied * lax.rsqrt(mean + rms_epsilon) * gain_ref[:, lanes]
            share = sigmoid(far_level[h, :1, rows] - near_level[h, :1, rows])
            share = jnp.broadcast_to(share, (HD, ROWS)).T
            near = near_ref[rows, lanes]
            attended = near + share * (far_ref[rows, lanes].astype(f32) - near)
            out_ref[rows, lanes] = (normed + attended).astype(bf16)
    done = pltpu.make_async_copy(out_ref, out_hbm.at[group], sems.at[7])
    done.start()
    done.wait()


def finish(group, so_far, queries, near, far, weights, gain):
    groups, tokens, width = queries.shape
    heads = width // HD
    everywhere = pl.BlockSpec(memory_space=pl.ANY)
    block = pltpu.VMEM((tokens, width), bf16)
    level = pltpu.VMEM((heads, 8, tokens), f32)
    return pl.pallas_call(
        functools.partial(finish_kernel, group),
        out_shape=jax.ShapeDtypeStruct(queries.shape, bf16),
        in_specs=[everywhere] * 8,
        out_specs=everywhere,
        input_output_aliases={0: 0},
        scratch_shapes=[
            block,
            pltpu.VMEM((tokens, width), f32),
            level,
            block,
            level,
            pltpu.VMEM(weights.shape, f32),
            pltpu.VMEM(gain.shape, f32),
            block,
            pltpu.SemaphoreType.DMA((8,)),
        ],
        compiler_params=pltpu.CompilerParams(vmem_limit_bytes=VMEM_LIMIT),
        cost_estimate=pl.CostEstimate(
            flops=heads * tokens * 6 * HD * FW,
            bytes_accessed=16 * tokens * width,
            transcendentals=heads * tokens * FW,
        ),
        name="finish",
    )(so_far, queries, *near, *far, weights, gain)


def add_kernel(x_ref, out_ref):
    total = jnp.sum(x_ref[...].astype(f32), axis=0).astype(bf16)
    for i in range(out_ref.shape[0]):
        out_ref[i] = total


def after(x, event):
    return lax.optimization_barrier((x, event))[0]


def exchange(tiles):
    return lax.all_to_all(tiles, "seq", 0, 0, tiled=True)


def add_parts(arrived):
    vmem = pl.BlockSpec(memory_space=pltpu.VMEM)
    return pl.pallas_call(
        add_kernel,
        out_shape=jax.ShapeDtypeStruct(arrived.shape, bf16),
        in_specs=[vmem],
        out_specs=vmem,
        compiler_params=pltpu.CompilerParams(vmem_limit_bytes=SMALL_LIMIT),
        name="add_parts",
    )(arrived)


def body(
    query_vectors,
    key_vectors,
    value_vectors,
    token_rates,
    gate_weight,
    up_weight,
    down_weight,
    step_sizes,
    norm_gain,
):
    rank = lax.axis_index("seq")
    size = lax.axis_size("seq")
    gain = norm_gain.reshape(1, -1)
    ranks = rank.astype(jnp.int32).reshape(1)

    def send(block, distance):
        return move(block, lambda i: (i + distance) % size)

    def swap(block):
        return move(block, lambda i: i ^ 1)

    together = lax.optimization_barrier
    first = (gate_weight, up_weight, down_weight)
    own = (query_vectors, key_vectors, value_vectors)
    far_keys = send(key_vectors[0], 2)
    weights, limits, partial = local_grads(
        0, key_vectors, value_vectors, token_rates, first, step_sizes
    )
    far_values = send(after(value_vectors[0], (far_keys, partial)), 2)
    asked = send(after(query_vectors[1], partial), -2)
    early = [swap(t) for t in own[1:]]
    arrived = exchange(partial.reshape(size, -1, HD))
    near = part(1, size, False, after(ranks, far_keys), *own, early)
    arrived, near = together((arrived, near))
    added = add_parts(arrived)
    summed = exchange(added)
    answer = part(1, size, True, ranks, after(asked, added), *own[1:], early)
    context = (far_keys, far_values, swap(far_keys), swap(far_values))
    summed, answer = together((summed, answer))
    far = [send(a, 2) for a in answer]
    later = step(summed.reshape(partial.shape), weights, limits)
    (partial,) = local_grads(1, key_vectors, value_vectors, token_rates, (later,))
    partial, far = together((partial, far))
    arrived = exchange(partial.reshape(size, -1, HD))
    mixed = mix(0, ranks, *own, early, context, weights, gain)
    arrived, mixed = together((arrived, mixed))
    summed = exchange(add_parts(arrived))
    mixed = finish(1, mixed, query_vectors, near, far, later, gain)
    summed, mixed = together((summed, mixed))
    last = step(summed.reshape(partial.shape), later, limits)
    return mixed, last


def solution(mesh):
    return jax.shard_map(
        body,
        mesh=mesh,
        in_specs=(
            P("batch", "seq", "head"),
            P("batch", "seq", "head"),
            P("batch", "seq", "head"),
            P("batch", "head", "seq"),
            P("head", None, None),
            P("head", None, None),
            P("head", None, None),
            P("head"),
            P("head"),
        ),
        out_specs=(P("batch", "seq", "head"), P("batch", "head", None, None)),
        check_vma=False,
    )
```

```python
import functools
import math

import jax
import jax.numpy as jnp
from jax import lax
from jax.experimental import pallas as pl
from jax.experimental.pallas import tpu as pltpu
from jax.sharding import PartitionSpec as P

HD = 128
FW = 256
NS_STEPS = 5
ROWS = 256

coeff_first = 3.4445
coeff_second = -4.775
coeff_third = 2.0315
frob_epsilon = 1e-07
rms_epsilon = 1e-06
column_epsilon = 1e-06

f32 = jnp.float32
bf16 = jnp.bfloat16
LEAST_SUM = 1e-25
MOST_SUM = 1e30
NO_KEYS = -1e30
VMEM_LIMIT = 62 * 1024 * 1024
SMALL_LIMIT = 24 * 1024 * 1024
STEP_LIMIT = 24 * 1024 * 1024
PART_LIMIT = 32 * 1024 * 1024


def dot(a, b, over=((1,), (0,))):
    return lax.dot_general(a, b, (over, ((), ())), preferred_element_type=f32)


def sigmoid(x):
    return 0.5 * jnp.tanh(0.5 * x) + 0.5


def move(block, route):
    return lax.ppermute(block, "seq", [(i, route(i)) for i in range(lax.axis_size("seq"))])


def fetch(copies, sems, at=0):
    started = [pltpu.make_async_copy(a, b, sems.at[at + i]) for i, (a, b) in enumerate(copies)]
    for copy in started:
        copy.start()
    return started


def fetch(copies, sems, at=0):
    started = [pltpu.make_async_copy(a, b, sems.at[at + i]) for i, (a, b) in enumerate(copies)]
    for copy in started:
        copy.start()
    return started


def grads_kernel(group, k_ref, v_ref, r_ref, *refs):
    if k_ref.ndim == 3:
        k_ref, v_ref, r_ref = k_ref.at[group], v_ref.at[group], r_ref.at[group]
    *w_refs, out_ref, grad_ref, hid_ref, og_ref = refs
    if len(w_refs) > 1:
        step_ref, *w_refs, kept_ref, limits_ref = w_refs
        for which in range(3):
            weight = w_refs[which][...]
            kept_ref[which] = weight
            limits_ref[which, :, :1] = jnp.sqrt(jnp.sum(weight * weight, axis=1, keepdims=True))
            for h in range(weight.shape[0]):
                limits_ref[which, h, 1:] = jnp.full((1, FW), step_ref[h], f32)
    else:
        w_refs = [w_refs[0].at[which] for which in range(3)]
    tokens, width = k_ref.shape
    for h in range(width // HD):
        lanes = slice(h * HD, (h + 1) * HD)
        low_gate, low_up, low_down = (w_ref[h].astype(bf16) for w_ref in w_refs)
        for c in range(tokens // ROWS):
            rows = slice(c * ROWS, (c + 1) * ROWS)
            keys = k_ref[rows, lanes]
            rate = jnp.broadcast_to(r_ref[h : h + 1, rows], (HD, ROWS)).T
            out_grad = (-rate * v_ref[rows, lanes].astype(f32)).astype(bf16)
            gate_pre = dot(keys, low_gate)
            up_pre = dot(keys, low_up)
            hidden_grad = dot(out_grad, low_down)
            sig = sigmoid(gate_pre)
            active = gate_pre * sig
            og_ref[rows] = out_grad
            hid_ref[rows] = (active * up_pre).astype(bf16)
            grad_ref[rows, FW:] = (hidden_grad * active).astype(bf16)
            grad_ref[rows, :FW] = (
                hidden_grad * up_pre * sig * (1.0 + gate_pre * (1.0 - sig))
            ).astype(bf16)
        both = dot(k_ref[:, lanes], grad_ref[...], ((0,), (0,)))
        down = dot(og_ref[...], hid_ref[...], ((0,), (0,)))
        for which, full in enumerate((both[:, :FW], both[:, FW:], down)):
            for half in range(2):
                out_ref[which, h, half] = full[:, half * HD : (half + 1) * HD].astype(bf16)


def local_grads(group, keys, values, rates, weights, step_sizes=None):
    _, tokens, width = keys.shape
    heads = width // HD
    vmem = pl.BlockSpec(memory_space=pltpu.VMEM)
    out_shape = [jax.ShapeDtypeStruct((3, heads, 2, HD, HD), bf16)]
    if step_sizes is None:
        extra, limit = [], SMALL_LIMIT
        in_specs = [vmem] * (3 + len(weights))
        out_specs = [vmem]
    else:
        extra, limit = [step_sizes], VMEM_LIMIT
        group_rows = pl.BlockSpec((None, tokens, width), lambda i: (group, 0, 0))
        in_specs = (
            [group_rows] * 2
            + [pl.BlockSpec((None, heads, tokens), lambda i: (group, 0, 0))]
            + [pl.BlockSpec(memory_space=pltpu.SMEM)]
            + [pl.BlockSpec((heads, HD, FW), lambda i: (0, 0, 0))] * len(weights)
        )
        out_shape = [
            jax.ShapeDtypeStruct((3, heads, HD, FW), f32),
            jax.ShapeDtypeStruct((3, heads, 2, FW), f32),
        ] + out_shape
        out_specs = [pl.BlockSpec(o.shape, lambda i, n=len(o.shape): (0,) * n) for o in out_shape]
    return pl.pallas_call(
        functools.partial(grads_kernel, group),
        out_shape=out_shape,
        grid=(1,) if extra else (),
        in_specs=in_specs,
        out_specs=out_specs,
        scratch_shapes=[
            pltpu.VMEM((tokens, 2 * FW), bf16),
            pltpu.VMEM((tokens, FW), bf16),
            pltpu.VMEM((tokens, HD), bf16),
        ],
        compiler_params=pltpu.CompilerParams(vmem_limit_bytes=limit),
        cost_estimate=pl.CostEstimate(
            flops=12 * heads * tokens * HD * FW,
            bytes_accessed=4 * tokens * width,
            transcendentals=heads * tokens * FW,
        ),
        name="local_grads",
    )(keys, values, rates, *extra, *weights)


def split(x):
    high = x.astype(bf16)
    return high, (x - high.astype(f32)).astype(bf16)


def sweeps(x_ref, count):
    def sweep(_, carry):
        pieces, grams, polynomials = [], [], []
        for m in range(count):
            high, low = split(x_ref[m])
            pieces.append((high, low))
            stacked = jnp.concatenate([high, low], axis=0)
            g = dot(stacked, stacked, ((1,), (1,)))
            grams.append(g[:HD, :HD] + (g[HD:, :HD] + g[:HD, HD:]) + g[HD:, HD:])
        for m in range(count):
            row = jnp.concatenate(split(grams[m]), axis=1)
            squared = dot(row, jnp.concatenate([row, row], axis=0))
            polynomials.append(
                coeff_second * grams[m] + coeff_third * (squared[:, :HD] + squared[:, HD:])
            )
        for m in range(count):
            high, low = pieces[m]
            row = jnp.concatenate(split(polynomials[m]), axis=1)
            product = dot(row, jnp.concatenate([high, high], axis=0)) + dot(
                row, jnp.concatenate([low, low], axis=0)
            )
            x_ref[m] = coeff_first * x_ref[m] + product
        return carry

    lax.fori_loop(0, NS_STEPS, sweep, 0)


def step_kernel(s_ref, w_hbm, limits_hbm, out_hbm, x_ref, w_ref, limits_ref, out_ref, sems):
    heads = out_ref.shape[1]
    started = fetch([(w_hbm, w_ref), (limits_hbm, limits_ref)], sems)
    for which in range(3):
        for h in range(heads):
            grad = jnp.concatenate([s_ref[which, h, 0], s_ref[which, h, 1]], axis=1).astype(f32)
            frobenius = jnp.sqrt(jnp.sum(grad * grad, keepdims=True))
            x_ref[which * heads + h] = grad / (frobenius + frob_epsilon)
    sweeps(x_ref, 3 * heads)
    for copy in started:
        copy.wait()
    written = []
    for which in range(3):
        for h in range(heads):
            target = limits_ref[which, h, :1]
            stepped = w_ref[which, h] - limits_ref[which, h, 1:] * x_ref[which * heads + h]
            length = jnp.sqrt(jnp.sum(stepped * stepped, axis=0, keepdims=True))
            out_ref[which, h] = stepped * (target / (length + column_epsilon))
        copy = pltpu.make_async_copy(out_ref.at[which], out_hbm.at[which], sems.at[2 + which])
        copy.start()
        written.append(copy)
    for copy in written:
        copy.wait()


def step(summed, weights, limits):
    heads = weights.shape[1]
    everywhere = pl.BlockSpec(memory_space=pl.ANY)
    return pl.pallas_call(
        step_kernel,
        out_shape=jax.ShapeDtypeStruct(weights.shape, f32),
        in_specs=[pl.BlockSpec(memory_space=pltpu.VMEM), everywhere, everywhere],
        out_specs=everywhere,
        scratch_shapes=[
            pltpu.VMEM((3 * heads, HD, FW), f32),
            pltpu.VMEM(weights.shape, f32),
            pltpu.VMEM(limits.shape, f32),
            pltpu.VMEM(weights.shape, f32),
            pltpu.SemaphoreType.DMA((5,)),
        ],
        compiler_params=pltpu.CompilerParams(vmem_limit_bytes=STEP_LIMIT),
        cost_estimate=pl.CostEstimate(
            flops=3 * heads * NS_STEPS * 40 * HD * HD * FW,
            bytes_accessed=3 * heads * 10 * HD * FW,
            transcendentals=0,
        ),
        name="weight_step",
    )(summed, weights, limits)


def mix_kernel(group, rank_ref, *refs):
    (
        q_hbm, k_hbm, v_hbm, ks_hbm, vs_hbm, kf_hbm, vf_hbm, kb_hbm, vb_hbm, w_hbm, gain_hbm,
        out_hbm, q_ref, ko_ref, vo_ref, kf_ref, vf_ref, kn_ref, vn_ref, w_ref, gain_ref,
        normed_ref, out_ref, sems,
    ) = refs
    tokens, width = q_ref.shape
    heads = width // HD
    scale = 1.0 / math.sqrt(HD)
    power = scale * math.log2(math.e)
    blocks = tokens // ROWS
    odd = rank_ref[0] % 2 == 1
    started = fetch(
        [
            (w_hbm, w_ref),
            (gain_hbm, gain_ref),
            (q_hbm.at[group], q_ref),
            (k_hbm.at[group], ko_ref),
            (v_hbm.at[group], vo_ref),
            (kf_hbm, kf_ref),
            (vf_hbm, vf_ref),
        ],
        sems,
    )
    beside = [(ks_hbm.at[group], kn_ref), (vs_hbm.at[group], vn_ref)]
    behind = [(kb_hbm, kn_ref), (vb_hbm, vn_ref)]

    @pl.when(odd)
    def _():
        fetch(beside, sems, 7)

    @pl.when(jnp.logical_not(odd))
    def _():
        fetch(behind, sems, 7)

    started += [pltpu.make_async_copy(a, b, sems.at[7 + i]) for i, (a, b) in enumerate(behind)]
    for copy in started[:3]:
        copy.wait()
    all_lanes = [slice(h * HD, (h + 1) * HD) for h in range(heads)]
    all_rows = [slice(b * ROWS, (b + 1) * ROWS) for b in range(blocks)]
    for h, lanes in enumerate(all_lanes):
        low_gate, low_up, low_down = (w_ref[which, h].astype(bf16) for which in range(3))
        for rows in all_rows:
            q = q_ref[rows, lanes]
            gate_pre = dot(q, low_gate)
            hidden = (gate_pre * sigmoid(gate_pre) * dot(q, low_up)).astype(bf16)
            applied = dot(hidden, low_down, ((1,), (1,)))
            mean = jnp.mean(applied * applied, axis=1, keepdims=True)
            normed_ref[rows, lanes] = applied * lax.rsqrt(mean + rms_epsilon) * gain_ref[:, lanes]
    for copy in started[3:]:
        copy.wait()

    near_valid = rank_ref[0] >= 1 if group == 0 else True
    far_valid = rank_ref[0] >= 2 if group == 0 else True

    def beside_ones(v, valid=True):
        wide = jnp.concatenate([v, jnp.ones((v.shape[0], HD), bf16)], axis=1)
        return wide if valid is True else wide * jnp.where(valid, 1.0, 0.0).astype(bf16)

    causal = lax.broadcasted_iota(jnp.int32, (ROWS, ROWS), 0) >= lax.broadcasted_iota(
        jnp.int32, (ROWS, ROWS), 1
    )

    def raised(q, keys):
        return jnp.exp2(dot(q, keys, ((1,), (1,))) * power).astype(bf16)

    wrong = jnp.zeros((ROWS, HD), f32)
    for lanes in all_lanes:
        for b, rows in enumerate(all_rows):
            q = q_ref[rows, lanes]
            own = dot(q, ko_ref[rows, lanes], ((1,), (1,)))
            far = dot(q, kf_ref[rows, lanes], ((1,), (1,)))
            edge = jnp.exp2(jnp.where(causal, own, far) * power)
            total = dot(
                jnp.where(causal, edge, 0.0).astype(bf16), beside_ones(vo_ref[rows, lanes])
            )
            total += dot(
                jnp.where(causal, 0.0, edge).astype(bf16),
                beside_ones(vf_ref[rows, lanes], far_valid),
            )
            total += dot(raised(q, kn_ref[:, lanes]), beside_ones(vn_ref[:, lanes], near_valid))
            if b > 0:
                past = slice(0, b * ROWS)
                total += dot(raised(q, ko_ref[past, lanes]), beside_ones(vo_ref[past, lanes]))
            if b < blocks - 1:
                rest = slice((b + 1) * ROWS, tokens)
                total += dot(
                    raised(q, kf_ref[rest, lanes]), beside_ones(vf_ref[rest, lanes], far_valid)
                )
            sums = total[:, HD:]
            out_ref[rows, lanes] = (normed_ref[rows, lanes] + total[:, :HD] / sums).astype(bf16)
            fine = (sums > LEAST_SUM) & (sums < MOST_SUM)
            wrong = jnp.maximum(wrong, jnp.where(fine, 0.0, 1.0))

    @pl.when(jnp.max(wrong) > 0.0)
    def _():
        def one_block(b, carry):
            rows = pl.ds(pl.multiple_of(b * ROWS, ROWS), ROWS)
            place = b * ROWS + lax.broadcasted_iota(jnp.int32, (ROWS, tokens), 0)
            column = lax.broadcasted_iota(jnp.int32, (ROWS, tokens), 1)
            limit = jnp.where(far_valid, tokens, -1)
            least = jnp.where(near_valid, 0, tokens)
            lowest = jnp.float32(-jnp.inf)
            for lanes in all_lanes:
                q = q_ref[rows, lanes]
                far = dot(q, kf_ref[:, lanes], ((1,), (1,))) * scale
                far = jnp.where((column > place) & (column < limit), far, lowest)
                near = dot(q, kn_ref[:, lanes], ((1,), (1,))) * scale
                near = jnp.where(column >= least, near, lowest)
                own = dot(q, ko_ref[:, lanes], ((1,), (1,))) * scale
                own = jnp.where(column <= place, own, lowest)
                parts = ((far, vf_ref), (near, vn_ref), (own, vo_ref))
                most = jnp.max(own, axis=1, keepdims=True)
                for scores, _ in parts[:2]:
                    most = jnp.maximum(most, jnp.max(scores, axis=1, keepdims=True))
                total = jnp.zeros((ROWS, HD), f32)
                sums = jnp.zeros((ROWS, 1), f32)
                for scores, v_ref in parts:
                    e = jnp.exp(scores - most)
                    sums += jnp.sum(e, axis=1, keepdims=True)
                    total += dot(e.astype(bf16), v_ref[:, lanes])
                out_ref[rows, lanes] = (normed_ref[rows, lanes] + total / sums).astype(bf16)
            return carry

        lax.fori_loop(0, blocks, one_block, 0)

    done = pltpu.make_async_copy(out_ref, out_hbm.at[group], sems.at[9])
    done.start()
    done.wait()


def mix(group, rank, queries, keys, values, early, context, weights, gain):
    groups, tokens, width = queries.shape
    heads = width // HD
    everywhere = pl.BlockSpec(memory_space=pl.ANY)
    block = pltpu.VMEM((tokens, width), bf16)
    return pl.pallas_call(
        functools.partial(mix_kernel, group),
        out_shape=jax.ShapeDtypeStruct(queries.shape, bf16),
        in_specs=[pl.BlockSpec(memory_space=pltpu.SMEM)] + [everywhere] * 11,
        out_specs=everywhere,
        scratch_shapes=[block] * 7
        + [
            pltpu.VMEM(weights.shape, f32),
            pltpu.VMEM(gain.shape, f32),
            pltpu.VMEM((tokens, width), f32),
            block,
            pltpu.SemaphoreType.DMA((10,)),
        ],
        compiler_params=pltpu.CompilerParams(vmem_limit_bytes=VMEM_LIMIT),
        cost_estimate=pl.CostEstimate(
            flops=heads * tokens * 2 * tokens * 8 * HD,
            bytes_accessed=16 * tokens * width,
            transcendentals=heads * tokens * 2 * tokens,
        ),
        name="mix",
    )(rank, queries, keys, values, *early, *context, weights, gain)


def raise_to(q, keys):
    power = math.log2(math.e) / math.sqrt(HD)
    return jnp.exp2(dot(q, keys, ((1,), (1,))) * power)


def with_ones(v):
    return jnp.concatenate([v, jnp.ones((v.shape[0], HD), bf16)], axis=1)


def weighted(e, v):
    return dot(e.astype(bf16), with_ones(v))


def from_maximum(q, parts):
    scores = []
    most = jnp.full((q.shape[0], 1), NO_KEYS, f32)
    for keys, _, allowed in parts:
        s = dot(q, keys, ((1,), (1,))) / math.sqrt(HD)
        scores.append(s)
        most = jnp.maximum(
            most, jnp.max(jnp.where(allowed, s, NO_KEYS), axis=1, keepdims=True)
        )
    total = jnp.zeros((q.shape[0], HD), f32)
    sums = jnp.zeros((q.shape[0], 1), f32)
    for s, (_, values, allowed) in zip(scores, parts):
        e = jnp.where(allowed, jnp.exp(jnp.where(allowed, s, most) - most), 0.0)
        sums += jnp.sum(e, axis=1, keepdims=True)
        total += dot(e.astype(bf16), values)
    some = sums > 0.0
    safe = jnp.where(some, sums, 1.0)
    level = jnp.where(some, most + jnp.log(safe), NO_KEYS)
    return total / safe, jnp.broadcast_to(level, total.shape)


def unsafe(sums):
    return jnp.where((sums > LEAST_SUM) & (sums < MOST_SUM), 0.0, 1.0)


def places(first_row, tokens):
    row = first_row + lax.broadcasted_iota(jnp.int32, (ROWS, tokens), 0)
    return row, lax.broadcasted_iota(jnp.int32, (ROWS, tokens), 1)


def remote_kernel(group, size, rank_ref, *refs):
    (
        q_hbm, k_hbm, v_hbm, ks_hbm, vs_hbm, out_ref, level_ref,
        q_ref, ko_ref, vo_ref, ks_ref, vs_ref, total_ref, sems,
    ) = refs
    tokens, width = q_ref.shape
    heads = width // HD
    blocks = tokens // ROWS
    rank = rank_ref[0]
    even = rank % 2 == 0
    at = jnp.where(rank >= size - 2, group - 1, group)
    started = fetch(
        [
            (q_hbm, q_ref),
            (k_hbm.at[at], ko_ref),
            (v_hbm.at[at], vo_ref),
            (ks_hbm.at[at], ks_ref),
            (vs_hbm.at[at], vs_ref),
        ],
        sems,
    )
    for copy in started[:3]:
        copy.wait()
    all_lanes = [slice(h * HD, (h + 1) * HD) for h in range(heads)]
    all_rows = [slice(b * ROWS, (b + 1) * ROWS) for b in range(blocks)]
    row, column = places(0, ROWS)
    for h, lanes in enumerate(all_lanes):
        for b, rows in enumerate(all_rows):
            q = q_ref[rows, lanes]
            e = jnp.where(column > row, raise_to(q, ko_ref[rows, lanes]), 0.0)
            total = weighted(e, vo_ref[rows, lanes])
            if b < blocks - 1:
                rest = slice((b + 1) * ROWS, tokens)
                total += weighted(raise_to(q, ko_ref[rest, lanes]), vo_ref[rest, lanes])
            total_ref[h, rows] = total
    for copy in started[3:]:
        copy.wait()

    @pl.when(even)
    def _():
        for h, lanes in enumerate(all_lanes):
            for rows in all_rows:
                e = raise_to(q_ref[rows, lanes], ks_ref[:, lanes])
                total_ref[h, rows] += weighted(e, vs_ref[:, lanes])

    wrong = jnp.zeros((ROWS, HD), f32)
    for h, lanes in enumerate(all_lanes):
        for b, rows in enumerate(all_rows):
            total = total_ref[h, rows]
            sums = total[:, HD:]
            some = sums > 0.0
            safe = jnp.where(some, sums, 1.0)
            out_ref[rows, lanes] = (total[:, :HD] / safe).astype(bf16)
            level = jnp.where(some, jnp.log(safe), NO_KEYS)
            level_ref[h, :, rows] = level.T[:8]
            bad = unsafe(sums)
            if b == blocks - 1:
                last = lax.broadcasted_iota(jnp.int32, bad.shape, 0) == ROWS - 1
                bad = jnp.where(last & jnp.logical_not(even), 0.0, bad)
            wrong = jnp.maximum(wrong, bad)

    @pl.when(jnp.max(wrong) > 0.0)
    def _():
        def one_block(b, carry):
            rows = pl.ds(pl.multiple_of(b * ROWS, ROWS), ROWS)
            row, column = places(b * ROWS, tokens)
            everyone = column >= jnp.where(even, 0, tokens)
            for h, lanes in enumerate(all_lanes):
                parts = (
                    (ko_ref[:, lanes], vo_ref[:, lanes], column > row),
                    (ks_ref[:, lanes], vs_ref[:, lanes], everyone),
                )
                values, level = from_maximum(q_ref[rows, lanes], parts)
                out_ref[rows, lanes] = values.astype(bf16)
                level_ref[h, :, rows] = level.T[:8]
            return carry

        lax.fori_loop(0, blocks, one_block, 0)


def remote_part(group, size, rank, received, keys, values, early):
    tokens, width = received.shape
    heads = width // HD
    everywhere = pl.BlockSpec(memory_space=pl.ANY)
    block = pltpu.VMEM((tokens, width), bf16)
    return pl.pallas_call(
        functools.partial(remote_kernel, group, size),
        out_shape=[
            jax.ShapeDtypeStruct((tokens, width), bf16),
            jax.ShapeDtypeStruct((heads, 8, tokens), f32),
        ],
        in_specs=[pl.BlockSpec(memory_space=pltpu.SMEM)] + [everywhere] * 5,
        out_specs=[pl.BlockSpec()] * 2,
        scratch_shapes=[block] * 5
        + [pltpu.VMEM((heads, tokens, 2 * HD), f32), pltpu.SemaphoreType.DMA((5,))],
        compiler_params=pltpu.CompilerParams(vmem_limit_bytes=PART_LIMIT),
        cost_estimate=pl.CostEstimate(
            flops=heads * tokens * tokens * 8 * HD,
            bytes_accessed=12 * tokens * width,
            transcendentals=heads * tokens * tokens,
        ),
        name="remote_part",
    )(rank, received, keys, values, *early)


def finish_kernel(group, _, rank_ref, *refs):
    (
        q_hbm, k_hbm, v_hbm, ks_hbm, vs_hbm, o_hbm, level_hbm, w_hbm, gain_hbm, out_hbm,
        q_ref, ko_ref, vo_ref, ks_ref, vs_ref, o_ref, level_ref, w_ref, gain_ref,
        normed_ref, total_ref, out_ref, sems,
    ) = refs
    tokens, width = q_ref.shape
    heads = width // HD
    blocks = tokens // ROWS
    odd = rank_ref[0] % 2 == 1
    started = fetch(
        [
            (w_hbm, w_ref),
            (gain_hbm, gain_ref),
            (q_hbm.at[group], q_ref),
            (k_hbm.at[group], ko_ref),
            (v_hbm.at[group], vo_ref),
            (ks_hbm.at[group], ks_ref),
            (vs_hbm.at[group], vs_ref),
            (o_hbm, o_ref),
            (level_hbm, level_ref),
        ],
        sems,
    )
    for copy in started[:3]:
        copy.wait()
    all_lanes = [slice(h * HD, (h + 1) * HD) for h in range(heads)]
    all_rows = [slice(b * ROWS, (b + 1) * ROWS) for b in range(blocks)]
    for h, lanes in enumerate(all_lanes):
        low_gate, low_up, low_down = (w_ref[which, h].astype(bf16) for which in range(3))
        for rows in all_rows:
            q = q_ref[rows, lanes]
            gate_pre = dot(q, low_gate)
            hidden = (gate_pre * sigmoid(gate_pre) * dot(q, low_up)).astype(bf16)
            applied = dot(hidden, low_down, ((1,), (1,)))
            mean = jnp.mean(applied * applied, axis=1, keepdims=True)
            normed_ref[rows, lanes] = applied * lax.rsqrt(mean + rms_epsilon) * gain_ref[:, lanes]
    for copy in started[3:]:
        copy.wait()
    row, column = places(0, ROWS)
    for h, lanes in enumerate(all_lanes):
        for b, rows in enumerate(all_rows):
            q = q_ref[rows, lanes]
            e = jnp.where(column <= row, raise_to(q, ko_ref[rows, lanes]), 0.0)
            total = weighted(e, vo_ref[rows, lanes])
            if b > 0:
                past = slice(0, b * ROWS)
                total += weighted(raise_to(q, ko_ref[past, lanes]), vo_ref[past, lanes])
            total_ref[h, rows] = total

    @pl.when(odd)
    def _():
        for h, lanes in enumerate(all_lanes):
            for rows in all_rows:
                e = raise_to(q_ref[rows, lanes], ks_ref[:, lanes])
                total_ref[h, rows] += weighted(e, vs_ref[:, lanes])

    def joined(rows, lanes, h, values, level):
        other = jnp.broadcast_to(level_ref[h, :1, rows], (HD, ROWS)).T
        share = sigmoid(other - level)
        attended = values + share * (o_ref[rows, lanes].astype(f32) - values)
        return (normed_ref[rows, lanes] + attended).astype(bf16)

    wrong = jnp.zeros((ROWS, HD), f32)
    for h, lanes in enumerate(all_lanes):
        for rows in all_rows:
            total = total_ref[h, rows]
            sums = total[:, HD:]
            out_ref[rows, lanes] = joined(rows, lanes, h, total[:, :HD] / sums, jnp.log(sums))
            wrong = jnp.maximum(wrong, unsafe(sums))

    @pl.when(jnp.max(wrong) > 0.0)
    def _():
        def one_block(b, carry):
            rows = pl.ds(pl.multiple_of(b * ROWS, ROWS), ROWS)
            row, column = places(b * ROWS, tokens)
            everyone = column >= jnp.where(odd, 0, tokens)
            for h, lanes in enumerate(all_lanes):
                parts = (
                    (ko_ref[:, lanes], vo_ref[:, lanes], column <= row),
                    (ks_ref[:, lanes], vs_ref[:, lanes], everyone),
                )
                values, level = from_maximum(q_ref[rows, lanes], parts)
                out_ref[rows, lanes] = joined(rows, lanes, h, values, level)
            return carry

        lax.fori_loop(0, blocks, one_block, 0)

    done = pltpu.make_async_copy(out_ref, out_hbm.at[group], sems.at[9])
    done.start()
    done.wait()


def finish(group, so_far, rank, queries, keys, values, early, far, weights, gain):
    groups, tokens, width = queries.shape
    heads = width // HD
    everywhere = pl.BlockSpec(memory_space=pl.ANY)
    block = pltpu.VMEM((tokens, width), bf16)
    return pl.pallas_call(
        functools.partial(finish_kernel, group),
        out_shape=jax.ShapeDtypeStruct(queries.shape, bf16),
        in_specs=[everywhere, pl.BlockSpec(memory_space=pltpu.SMEM)] + [everywhere] * 9,
        out_specs=everywhere,
        input_output_aliases={0: 0},
        scratch_shapes=[block] * 6
        + [
            pltpu.VMEM((heads, 8, tokens), f32),
            pltpu.VMEM(weights.shape, f32),
            pltpu.VMEM(gain.shape, f32),
            pltpu.VMEM((tokens, width), f32),
            pltpu.VMEM((heads, tokens, 2 * HD), f32),
            block,
            pltpu.SemaphoreType.DMA((10,)),
        ],
        compiler_params=pltpu.CompilerParams(vmem_limit_bytes=VMEM_LIMIT),
        cost_estimate=pl.CostEstimate(
            flops=heads * tokens * tokens * 14 * HD,
            bytes_accessed=16 * tokens * width,
            transcendentals=heads * tokens * 2 * tokens,
        ),
        name="finish",
    )(so_far, rank, queries, keys, values, *early, *far, weights, gain)


def add_kernel(x_ref, out_ref):
    total = jnp.sum(x_ref[...].astype(f32), axis=0).astype(bf16)
    for i in range(out_ref.shape[0]):
        out_ref[i] = total


def after(x, event):
    return lax.optimization_barrier((x, event))[0]


def exchange(tiles):
    return lax.all_to_all(tiles, "seq", 0, 0, tiled=True)


def add_parts(arrived):
    vmem = pl.BlockSpec(memory_space=pltpu.VMEM)
    return pl.pallas_call(
        add_kernel,
        out_shape=jax.ShapeDtypeStruct(arrived.shape, bf16),
        in_specs=[vmem],
        out_specs=vmem,
        compiler_params=pltpu.CompilerParams(vmem_limit_bytes=SMALL_LIMIT),
        name="add_parts",
    )(arrived)


def body(
    query_vectors,
    key_vectors,
    value_vectors,
    token_rates,
    gate_weight,
    up_weight,
    down_weight,
    step_sizes,
    norm_gain,
):
    rank = lax.axis_index("seq")
    size = lax.axis_size("seq")
    gain = norm_gain.reshape(1, -1)
    ranks = rank.astype(jnp.int32).reshape(1)

    def send(block, distance):
        return move(block, lambda i: (i + distance) % size)

    def swap(block):
        return move(block, lambda i: i ^ 1)

    together = lax.optimization_barrier
    first = (gate_weight, up_weight, down_weight)
    own = (query_vectors, key_vectors, value_vectors)
    far_keys = send(key_vectors[0], 2)
    weights, limits, partial = local_grads(
        0, key_vectors, value_vectors, token_rates, first, step_sizes
    )
    far_values = send(after(value_vectors[0], (far_keys, partial)), 2)
    asked = send(after(query_vectors[1], partial), -2)
    early = [swap(t) for t in own[1:]]
    added = add_parts(exchange(partial.reshape(size, -1, HD)))
    summed = exchange(added)
    answer = remote_part(1, size, ranks, after(asked, added), *own[1:], early)
    context = (far_keys, far_values, swap(far_keys), swap(far_values))
    summed, answer = together((summed, answer))
    far = [send(a, 2) for a in answer]
    later = step(summed.reshape(partial.shape), weights, limits)
    (partial,) = local_grads(1, key_vectors, value_vectors, token_rates, (later,))
    arrived = exchange(partial.reshape(size, -1, HD))
    mixed = mix(0, ranks, *own, early, context, weights, gain)
    arrived, mixed = together((arrived, mixed))
    summed = exchange(add_parts(arrived))
    mixed = finish(1, mixed, ranks, *own, early, far, later, gain)
    summed, mixed = together((summed, mixed))
    last = step(summed.reshape(partial.shape), later, limits)
    return mixed, last


def solution(mesh):
    return jax.shard_map(
        body,
        mesh=mesh,
        in_specs=(
            P("batch", "seq", "head"),
            P("batch", "seq", "head"),
            P("batch", "seq", "head"),
            P("batch", "head", "seq"),
            P("head", None, None),
            P("head", None, None),
            P("head", None, None),
            P("head"),
            P("head"),
        ),
        out_specs=(P("batch", "seq", "head"), P("batch", "head", None, None)),
        check_vma=False,
    )
```

```python
import functools
import math

import jax
import jax.numpy as jnp
from jax import lax
from jax.experimental import pallas as pl
from jax.experimental.pallas import tpu as pltpu
from jax.sharding import PartitionSpec as P

HD = 128
FW = 256
NS_STEPS = 5
ROWS = 256
SLOW_ROWS = 128
SLOW_MIX = 64

coeff_first = 3.4445
coeff_second = -4.775
coeff_third = 2.0315
frob_epsilon = 1e-07
rms_epsilon = 1e-06
column_epsilon = 1e-06

f32 = jnp.float32
bf16 = jnp.bfloat16
LEAST_SUM = 1e-25
MOST_SUM = 1e30
NO_KEYS = -1e30
VMEM_LIMIT = 62 * 1024 * 1024
SMALL_LIMIT = 24 * 1024 * 1024
STEP_LIMIT = 24 * 1024 * 1024
PART_LIMIT = 32 * 1024 * 1024


def dot(a, b, over=((1,), (0,))):
    return lax.dot_general(a, b, (over, ((), ())), preferred_element_type=f32)


def sigmoid(x):
    return 0.5 * jnp.tanh(0.5 * x) + 0.5


def move(block, route):
    return lax.ppermute(block, "seq", [(i, route(i)) for i in range(lax.axis_size("seq"))])


def fetch(copies, sems, at=0):
    started = [pltpu.make_async_copy(a, b, sems.at[at + i]) for i, (a, b) in enumerate(copies)]
    for copy in started:
        copy.start()
    return started


def fetch(copies, sems, at=0):
    started = [pltpu.make_async_copy(a, b, sems.at[at + i]) for i, (a, b) in enumerate(copies)]
    for copy in started:
        copy.start()
    return started


def grads_kernel(group, k_ref, v_ref, r_ref, *refs):
    if k_ref.ndim == 3:
        k_ref, v_ref, r_ref = k_ref.at[group], v_ref.at[group], r_ref.at[group]
    *w_refs, out_ref, grad_ref, hid_ref, og_ref = refs
    if len(w_refs) > 1:
        step_ref, *w_refs, kept_ref, limits_ref = w_refs
        for which in range(3):
            weight = w_refs[which][...]
            kept_ref[which] = weight
            limits_ref[which, :, :1] = jnp.sqrt(jnp.sum(weight * weight, axis=1, keepdims=True))
            for h in range(weight.shape[0]):
                limits_ref[which, h, 1:] = jnp.full((1, FW), step_ref[h], f32)
    else:
        w_refs = [w_refs[0].at[which] for which in range(3)]
    tokens, width = k_ref.shape
    for h in range(width // HD):
        lanes = slice(h * HD, (h + 1) * HD)
        low_gate, low_up, low_down = (w_ref[h].astype(bf16) for w_ref in w_refs)
        for c in range(tokens // ROWS):
            rows = slice(c * ROWS, (c + 1) * ROWS)
            keys = k_ref[rows, lanes]
            rate = jnp.broadcast_to(r_ref[h : h + 1, rows], (HD, ROWS)).T
            out_grad = (-rate * v_ref[rows, lanes].astype(f32)).astype(bf16)
            gate_pre = dot(keys, low_gate)
            up_pre = dot(keys, low_up)
            hidden_grad = dot(out_grad, low_down)
            sig = sigmoid(gate_pre)
            active = gate_pre * sig
            og_ref[rows] = out_grad
            hid_ref[rows] = (active * up_pre).astype(bf16)
            grad_ref[rows, FW:] = (hidden_grad * active).astype(bf16)
            grad_ref[rows, :FW] = (
                hidden_grad * up_pre * sig * (1.0 + gate_pre * (1.0 - sig))
            ).astype(bf16)
        both = dot(k_ref[:, lanes], grad_ref[...], ((0,), (0,)))
        down = dot(og_ref[...], hid_ref[...], ((0,), (0,)))
        for which, full in enumerate((both[:, :FW], both[:, FW:], down)):
            for half in range(2):
                out_ref[which, h, half] = full[:, half * HD : (half + 1) * HD].astype(bf16)


def local_grads(group, keys, values, rates, weights, step_sizes=None):
    _, tokens, width = keys.shape
    heads = width // HD
    vmem = pl.BlockSpec(memory_space=pltpu.VMEM)
    out_shape = [jax.ShapeDtypeStruct((3, heads, 2, HD, HD), bf16)]
    if step_sizes is None:
        extra, limit = [], SMALL_LIMIT
        in_specs = [vmem] * (3 + len(weights))
        out_specs = [vmem]
    else:
        extra, limit = [step_sizes], VMEM_LIMIT
        group_rows = pl.BlockSpec((None, tokens, width), lambda i: (group, 0, 0))
        in_specs = (
            [group_rows] * 2
            + [pl.BlockSpec((None, heads, tokens), lambda i: (group, 0, 0))]
            + [pl.BlockSpec(memory_space=pltpu.SMEM)]
            + [pl.BlockSpec((heads, HD, FW), lambda i: (0, 0, 0))] * len(weights)
        )
        out_shape = [
            jax.ShapeDtypeStruct((3, heads, HD, FW), f32),
            jax.ShapeDtypeStruct((3, heads, 2, FW), f32),
        ] + out_shape
        out_specs = [pl.BlockSpec(o.shape, lambda i, n=len(o.shape): (0,) * n) for o in out_shape]
    return pl.pallas_call(
        functools.partial(grads_kernel, group),
        out_shape=out_shape,
        grid=(1,) if extra else (),
        in_specs=in_specs,
        out_specs=out_specs,
        scratch_shapes=[
            pltpu.VMEM((tokens, 2 * FW), bf16),
            pltpu.VMEM((tokens, FW), bf16),
            pltpu.VMEM((tokens, HD), bf16),
        ],
        compiler_params=pltpu.CompilerParams(vmem_limit_bytes=limit),
        cost_estimate=pl.CostEstimate(
            flops=12 * heads * tokens * HD * FW,
            bytes_accessed=4 * tokens * width,
            transcendentals=heads * tokens * FW,
        ),
        name="local_grads",
    )(keys, values, rates, *extra, *weights)


def split(x):
    high = x.astype(bf16)
    return high, (x - high.astype(f32)).astype(bf16)


def sweeps(x_ref, count):
    def sweep(_, carry):
        pieces, grams, polynomials = [], [], []
        for m in range(count):
            high, low = split(x_ref[m])
            pieces.append((high, low))
            stacked = jnp.concatenate([high, low], axis=0)
            g = dot(stacked, stacked, ((1,), (1,)))
            grams.append(g[:HD, :HD] + (g[HD:, :HD] + g[:HD, HD:]) + g[HD:, HD:])
        for m in range(count):
            row = jnp.concatenate(split(grams[m]), axis=1)
            squared = dot(row, jnp.concatenate([row, row], axis=0))
            polynomials.append(
                coeff_second * grams[m] + coeff_third * (squared[:, :HD] + squared[:, HD:])
            )
        for m in range(count):
            high, low = pieces[m]
            row = jnp.concatenate(split(polynomials[m]), axis=1)
            product = dot(row, jnp.concatenate([high, high], axis=0)) + dot(
                row, jnp.concatenate([low, low], axis=0)
            )
            x_ref[m] = coeff_first * x_ref[m] + product
        return carry

    lax.fori_loop(0, NS_STEPS, sweep, 0)


def step_kernel(s_ref, w_hbm, limits_hbm, out_hbm, x_ref, w_ref, limits_ref, out_ref, sems):
    heads = out_ref.shape[1]
    started = fetch([(w_hbm, w_ref), (limits_hbm, limits_ref)], sems)
    for which in range(3):
        for h in range(heads):
            grad = jnp.concatenate([s_ref[which, h, 0], s_ref[which, h, 1]], axis=1).astype(f32)
            frobenius = jnp.sqrt(jnp.sum(grad * grad, keepdims=True))
            x_ref[which * heads + h] = grad / (frobenius + frob_epsilon)
    sweeps(x_ref, 3 * heads)
    for copy in started:
        copy.wait()
    written = []
    for which in range(3):
        for h in range(heads):
            target = limits_ref[which, h, :1]
            stepped = w_ref[which, h] - limits_ref[which, h, 1:] * x_ref[which * heads + h]
            length = jnp.sqrt(jnp.sum(stepped * stepped, axis=0, keepdims=True))
            out_ref[which, h] = stepped * (target / (length + column_epsilon))
        copy = pltpu.make_async_copy(out_ref.at[which], out_hbm.at[which], sems.at[2 + which])
        copy.start()
        written.append(copy)
    for copy in written:
        copy.wait()


def step(summed, weights, limits):
    heads = weights.shape[1]
    everywhere = pl.BlockSpec(memory_space=pl.ANY)
    return pl.pallas_call(
        step_kernel,
        out_shape=jax.ShapeDtypeStruct(weights.shape, f32),
        in_specs=[pl.BlockSpec(memory_space=pltpu.VMEM), everywhere, everywhere],
        out_specs=everywhere,
        scratch_shapes=[
            pltpu.VMEM((3 * heads, HD, FW), f32),
            pltpu.VMEM(weights.shape, f32),
            pltpu.VMEM(limits.shape, f32),
            pltpu.VMEM(weights.shape, f32),
            pltpu.SemaphoreType.DMA((5,)),
        ],
        compiler_params=pltpu.CompilerParams(vmem_limit_bytes=STEP_LIMIT),
        cost_estimate=pl.CostEstimate(
            flops=3 * heads * NS_STEPS * 40 * HD * HD * FW,
            bytes_accessed=3 * heads * 10 * HD * FW,
            transcendentals=0,
        ),
        name="weight_step",
    )(summed, weights, limits)


def mix_kernel(group, rank_ref, *refs):
    (
        q_hbm, k_hbm, v_hbm, ks_hbm, vs_hbm, kf_hbm, vf_hbm, kb_hbm, vb_hbm, w_hbm, gain_hbm,
        out_hbm, q_ref, ko_ref, vo_ref, kf_ref, vf_ref, kn_ref, vn_ref, w_ref, gain_ref,
        normed_ref, out_ref, sems,
    ) = refs
    tokens, width = q_ref.shape
    heads = width // HD
    scale = 1.0 / math.sqrt(HD)
    power = scale * math.log2(math.e)
    blocks = tokens // ROWS
    odd = rank_ref[0] % 2 == 1
    started = fetch(
        [
            (w_hbm, w_ref),
            (gain_hbm, gain_ref),
            (q_hbm.at[group], q_ref),
            (k_hbm.at[group], ko_ref),
            (v_hbm.at[group], vo_ref),
            (kf_hbm, kf_ref),
            (vf_hbm, vf_ref),
        ],
        sems,
    )
    beside = [(ks_hbm.at[group], kn_ref), (vs_hbm.at[group], vn_ref)]
    behind = [(kb_hbm, kn_ref), (vb_hbm, vn_ref)]

    @pl.when(odd)
    def _():
        fetch(beside, sems, 7)

    @pl.when(jnp.logical_not(odd))
    def _():
        fetch(behind, sems, 7)

    started += [pltpu.make_async_copy(a, b, sems.at[7 + i]) for i, (a, b) in enumerate(behind)]
    for copy in started[:3]:
        copy.wait()
    all_lanes = [slice(h * HD, (h + 1) * HD) for h in range(heads)]
    all_rows = [slice(b * ROWS, (b + 1) * ROWS) for b in range(blocks)]
    for h, lanes in enumerate(all_lanes):
        low_gate, low_up, low_down = (w_ref[which, h].astype(bf16) for which in range(3))
        for rows in all_rows:
            q = q_ref[rows, lanes]
            gate_pre = dot(q, low_gate)
            hidden = (gate_pre * sigmoid(gate_pre) * dot(q, low_up)).astype(bf16)
            applied = dot(hidden, low_down, ((1,), (1,)))
            mean = jnp.mean(applied * applied, axis=1, keepdims=True)
            normed_ref[rows, lanes] = applied * lax.rsqrt(mean + rms_epsilon) * gain_ref[:, lanes]
    for copy in started[3:]:
        copy.wait()

    near_valid = rank_ref[0] >= 1 if group == 0 else True
    far_valid = rank_ref[0] >= 2 if group == 0 else True

    def beside_ones(v, valid=True):
        wide = jnp.concatenate([v, jnp.ones((v.shape[0], HD), bf16)], axis=1)
        return wide if valid is True else wide * jnp.where(valid, 1.0, 0.0).astype(bf16)

    causal = lax.broadcasted_iota(jnp.int32, (ROWS, ROWS), 0) >= lax.broadcasted_iota(
        jnp.int32, (ROWS, ROWS), 1
    )

    def raised(q, keys):
        return jnp.exp2(dot(q, keys, ((1,), (1,))) * power).astype(bf16)

    wrong = jnp.zeros((ROWS, HD), f32)
    for lanes in all_lanes:
        for b, rows in enumerate(all_rows):
            q = q_ref[rows, lanes]
            own = dot(q, ko_ref[rows, lanes], ((1,), (1,)))
            far = dot(q, kf_ref[rows, lanes], ((1,), (1,)))
            edge = jnp.exp2(jnp.where(causal, own, far) * power)
            total = dot(
                jnp.where(causal, edge, 0.0).astype(bf16), beside_ones(vo_ref[rows, lanes])
            )
            total += dot(
                jnp.where(causal, 0.0, edge).astype(bf16),
                beside_ones(vf_ref[rows, lanes], far_valid),
            )
            total += dot(raised(q, kn_ref[:, lanes]), beside_ones(vn_ref[:, lanes], near_valid))
            if b > 0:
                past = slice(0, b * ROWS)
                total += dot(raised(q, ko_ref[past, lanes]), beside_ones(vo_ref[past, lanes]))
            if b < blocks - 1:
                rest = slice((b + 1) * ROWS, tokens)
                total += dot(
                    raised(q, kf_ref[rest, lanes]), beside_ones(vf_ref[rest, lanes], far_valid)
                )
            sums = total[:, HD:]
            out_ref[rows, lanes] = (normed_ref[rows, lanes] + total[:, :HD] / sums).astype(bf16)
            fine = (sums > LEAST_SUM) & (sums < MOST_SUM)
            wrong = jnp.maximum(wrong, jnp.where(fine, 0.0, 1.0))

    @pl.when(jnp.max(wrong) > 0.0)
    def _():
        def one_block(step, carry):
            h, b = step % heads, step // heads
            one_head = [pl.ds(pl.multiple_of(h * HD, HD), HD)]
            rows = pl.ds(pl.multiple_of(b * SLOW_MIX, SLOW_MIX), SLOW_MIX)
            place, column = places(b * SLOW_MIX, (SLOW_MIX, tokens))
            limit = jnp.where(far_valid, tokens, -1)
            least = jnp.where(near_valid, 0, tokens)
            lowest = jnp.float32(-jnp.inf)
            for lanes in one_head:
                q = q_ref[rows, lanes]
                far = dot(q, kf_ref[:, lanes], ((1,), (1,))) * scale
                far = jnp.where((column > place) & (column < limit), far, lowest)
                near = dot(q, kn_ref[:, lanes], ((1,), (1,))) * scale
                near = jnp.where(column >= least, near, lowest)
                own = dot(q, ko_ref[:, lanes], ((1,), (1,))) * scale
                own = jnp.where(column <= place, own, lowest)
                parts = ((far, vf_ref), (near, vn_ref), (own, vo_ref))
                most = jnp.max(own, axis=1, keepdims=True)
                for scores, _ in parts[:2]:
                    most = jnp.maximum(most, jnp.max(scores, axis=1, keepdims=True))
                total = jnp.zeros((SLOW_MIX, HD), f32)
                sums = jnp.zeros((SLOW_MIX, 1), f32)
                for scores, v_ref in parts:
                    e = jnp.exp(scores - most)
                    sums += jnp.sum(e, axis=1, keepdims=True)
                    total += dot(e.astype(bf16), v_ref[:, lanes])
                out_ref[rows, lanes] = (normed_ref[rows, lanes] + total / sums).astype(bf16)
            return carry

        lax.fori_loop(0, heads * (tokens // SLOW_MIX), one_block, 0)

    done = pltpu.make_async_copy(out_ref, out_hbm.at[group], sems.at[9])
    done.start()
    done.wait()


def mix(group, rank, queries, keys, values, early, context, weights, gain):
    groups, tokens, width = queries.shape
    heads = width // HD
    everywhere = pl.BlockSpec(memory_space=pl.ANY)
    block = pltpu.VMEM((tokens, width), bf16)
    return pl.pallas_call(
        functools.partial(mix_kernel, group),
        out_shape=jax.ShapeDtypeStruct(queries.shape, bf16),
        in_specs=[pl.BlockSpec(memory_space=pltpu.SMEM)] + [everywhere] * 11,
        out_specs=everywhere,
        scratch_shapes=[block] * 7
        + [
            pltpu.VMEM(weights.shape, f32),
            pltpu.VMEM(gain.shape, f32),
            pltpu.VMEM((tokens, width), f32),
            block,
            pltpu.SemaphoreType.DMA((10,)),
        ],
        compiler_params=pltpu.CompilerParams(vmem_limit_bytes=VMEM_LIMIT),
        cost_estimate=pl.CostEstimate(
            flops=heads * tokens * 2 * tokens * 8 * HD,
            bytes_accessed=16 * tokens * width,
            transcendentals=heads * tokens * 2 * tokens,
        ),
        name="mix",
    )(rank, queries, keys, values, *early, *context, weights, gain)


def raise_to(q, keys):
    power = math.log2(math.e) / math.sqrt(HD)
    return jnp.exp2(dot(q, keys, ((1,), (1,))) * power)


def with_ones(v):
    return jnp.concatenate([v, jnp.ones((v.shape[0], HD), bf16)], axis=1)


def weighted(e, v):
    return dot(e.astype(bf16), with_ones(v))


def from_maximum(q, parts):
    scores = []
    most = jnp.full((q.shape[0], 1), NO_KEYS, f32)
    for keys, _, allowed in parts:
        s = dot(q, keys, ((1,), (1,))) / math.sqrt(HD)
        scores.append(s)
        most = jnp.maximum(
            most, jnp.max(jnp.where(allowed, s, NO_KEYS), axis=1, keepdims=True)
        )
    total = jnp.zeros((q.shape[0], HD), f32)
    sums = jnp.zeros((q.shape[0], 1), f32)
    for s, (_, values, allowed) in zip(scores, parts):
        e = jnp.where(allowed, jnp.exp(jnp.where(allowed, s, most) - most), 0.0)
        sums += jnp.sum(e, axis=1, keepdims=True)
        total += dot(e.astype(bf16), values)
    some = sums > 0.0
    safe = jnp.where(some, sums, 1.0)
    level = jnp.where(some, most + jnp.log(safe), NO_KEYS)
    return total / safe, jnp.broadcast_to(level, total.shape)


def unsafe(sums):
    return jnp.where((sums > LEAST_SUM) & (sums < MOST_SUM), 0.0, 1.0)


def places(first_row, shape):
    row = first_row + lax.broadcasted_iota(jnp.int32, shape, 0)
    return row, lax.broadcasted_iota(jnp.int32, shape, 1)


def remote_kernel(group, size, rank_ref, *refs):
    (
        q_hbm, k_hbm, v_hbm, ks_hbm, vs_hbm, out_ref, level_ref,
        q_ref, ko_ref, vo_ref, ks_ref, vs_ref, total_ref, sems,
    ) = refs
    tokens, width = q_ref.shape
    heads = width // HD
    blocks = tokens // ROWS
    rank = rank_ref[0]
    even = rank % 2 == 0
    at = jnp.where(rank >= size - 2, group - 1, group)
    started = fetch(
        [
            (q_hbm, q_ref),
            (k_hbm.at[at], ko_ref),
            (v_hbm.at[at], vo_ref),
            (ks_hbm.at[at], ks_ref),
            (vs_hbm.at[at], vs_ref),
        ],
        sems,
    )
    for copy in started[:3]:
        copy.wait()
    all_lanes = [slice(h * HD, (h + 1) * HD) for h in range(heads)]
    all_rows = [slice(b * ROWS, (b + 1) * ROWS) for b in range(blocks)]
    row, column = places(0, (ROWS, ROWS))
    for h, lanes in enumerate(all_lanes):
        for b, rows in enumerate(all_rows):
            q = q_ref[rows, lanes]
            e = jnp.where(column > row, raise_to(q, ko_ref[rows, lanes]), 0.0)
            total = weighted(e, vo_ref[rows, lanes])
            if b < blocks - 1:
                rest = slice((b + 1) * ROWS, tokens)
                total += weighted(raise_to(q, ko_ref[rest, lanes]), vo_ref[rest, lanes])
            total_ref[h, rows] = total
    for copy in started[3:]:
        copy.wait()

    @pl.when(even)
    def _():
        for h, lanes in enumerate(all_lanes):
            for rows in all_rows:
                e = raise_to(q_ref[rows, lanes], ks_ref[:, lanes])
                total_ref[h, rows] += weighted(e, vs_ref[:, lanes])

    wrong = jnp.zeros((ROWS, HD), f32)
    for h, lanes in enumerate(all_lanes):
        for b, rows in enumerate(all_rows):
            total = total_ref[h, rows]
            sums = total[:, HD:]
            some = sums > 0.0
            safe = jnp.where(some, sums, 1.0)
            out_ref[rows, lanes] = (total[:, :HD] / safe).astype(bf16)
            level = jnp.where(some, jnp.log(safe), NO_KEYS)
            level_ref[h, :, rows] = level.T[:8]
            bad = unsafe(sums)
            if b == blocks - 1:
                last = lax.broadcasted_iota(jnp.int32, bad.shape, 0) == ROWS - 1
                bad = jnp.where(last & jnp.logical_not(even), 0.0, bad)
            wrong = jnp.maximum(wrong, bad)

    @pl.when(jnp.max(wrong) > 0.0)
    def _():
        def one_block(step, carry):
            h, b = step % heads, step // heads
            one_head = [(h, pl.ds(pl.multiple_of(h * HD, HD), HD))]
            rows = pl.ds(pl.multiple_of(b * SLOW_ROWS, SLOW_ROWS), SLOW_ROWS)
            row, column = places(b * SLOW_ROWS, (SLOW_ROWS, tokens))
            everyone = column >= jnp.where(even, 0, tokens)
            for h, lanes in one_head:
                parts = (
                    (ko_ref[:, lanes], vo_ref[:, lanes], column > row),
                    (ks_ref[:, lanes], vs_ref[:, lanes], everyone),
                )
                values, level = from_maximum(q_ref[rows, lanes], parts)
                out_ref[rows, lanes] = values.astype(bf16)
                level_ref[h, :, rows] = level.T[:8]
            return carry

        lax.fori_loop(0, heads * (tokens // SLOW_ROWS), one_block, 0)


def remote_part(group, size, rank, received, keys, values, early):
    tokens, width = received.shape
    heads = width // HD
    everywhere = pl.BlockSpec(memory_space=pl.ANY)
    block = pltpu.VMEM((tokens, width), bf16)
    return pl.pallas_call(
        functools.partial(remote_kernel, group, size),
        out_shape=[
            jax.ShapeDtypeStruct((tokens, width), bf16),
            jax.ShapeDtypeStruct((heads, 8, tokens), f32),
        ],
        in_specs=[pl.BlockSpec(memory_space=pltpu.SMEM)] + [everywhere] * 5,
        out_specs=[pl.BlockSpec()] * 2,
        scratch_shapes=[block] * 5
        + [pltpu.VMEM((heads, tokens, 2 * HD), f32), pltpu.SemaphoreType.DMA((5,))],
        compiler_params=pltpu.CompilerParams(vmem_limit_bytes=PART_LIMIT),
        cost_estimate=pl.CostEstimate(
            flops=heads * tokens * tokens * 8 * HD,
            bytes_accessed=12 * tokens * width,
            transcendentals=heads * tokens * tokens,
        ),
        name="remote_part",
    )(rank, received, keys, values, *early)


def finish_kernel(group, _, rank_ref, *refs):
    (
        q_hbm, k_hbm, v_hbm, ks_hbm, vs_hbm, o_hbm, level_hbm, w_hbm, gain_hbm, out_hbm,
        q_ref, ko_ref, vo_ref, ks_ref, vs_ref, o_ref, level_ref, w_ref, gain_ref,
        normed_ref, total_ref, out_ref, sems,
    ) = refs
    tokens, width = q_ref.shape
    heads = width // HD
    blocks = tokens // ROWS
    odd = rank_ref[0] % 2 == 1
    started = fetch(
        [
            (w_hbm, w_ref),
            (gain_hbm, gain_ref),
            (q_hbm.at[group], q_ref),
            (k_hbm.at[group], ko_ref),
            (v_hbm.at[group], vo_ref),
            (ks_hbm.at[group], ks_ref),
            (vs_hbm.at[group], vs_ref),
            (o_hbm, o_ref),
            (level_hbm, level_ref),
        ],
        sems,
    )
    for copy in started[:3]:
        copy.wait()
    all_lanes = [slice(h * HD, (h + 1) * HD) for h in range(heads)]
    all_rows = [slice(b * ROWS, (b + 1) * ROWS) for b in range(blocks)]
    for h, lanes in enumerate(all_lanes):
        low_gate, low_up, low_down = (w_ref[which, h].astype(bf16) for which in range(3))
        for rows in all_rows:
            q = q_ref[rows, lanes]
            gate_pre = dot(q, low_gate)
            hidden = (gate_pre * sigmoid(gate_pre) * dot(q, low_up)).astype(bf16)
            applied = dot(hidden, low_down, ((1,), (1,)))
            mean = jnp.mean(applied * applied, axis=1, keepdims=True)
            normed_ref[rows, lanes] = applied * lax.rsqrt(mean + rms_epsilon) * gain_ref[:, lanes]
    for copy in started[3:]:
        copy.wait()
    row, column = places(0, (ROWS, ROWS))
    for h, lanes in enumerate(all_lanes):
        for b, rows in enumerate(all_rows):
            q = q_ref[rows, lanes]
            e = jnp.where(column <= row, raise_to(q, ko_ref[rows, lanes]), 0.0)
            total = weighted(e, vo_ref[rows, lanes])
            if b > 0:
                past = slice(0, b * ROWS)
                total += weighted(raise_to(q, ko_ref[past, lanes]), vo_ref[past, lanes])
            total_ref[h, rows] = total

    @pl.when(odd)
    def _():
        for h, lanes in enumerate(all_lanes):
            for rows in all_rows:
                e = raise_to(q_ref[rows, lanes], ks_ref[:, lanes])
                total_ref[h, rows] += weighted(e, vs_ref[:, lanes])

    def joined(rows, lanes, h, values, level):
        other = jnp.broadcast_to(level_ref[h, :1, rows], (HD, values.shape[0])).T
        share = sigmoid(other - level)
        attended = values + share * (o_ref[rows, lanes].astype(f32) - values)
        return (normed_ref[rows, lanes] + attended).astype(bf16)

    wrong = jnp.zeros((ROWS, HD), f32)
    for h, lanes in enumerate(all_lanes):
        for rows in all_rows:
            total = total_ref[h, rows]
            sums = total[:, HD:]
            out_ref[rows, lanes] = joined(rows, lanes, h, total[:, :HD] / sums, jnp.log(sums))
            wrong = jnp.maximum(wrong, unsafe(sums))

    @pl.when(jnp.max(wrong) > 0.0)
    def _():
        def one_block(step, carry):
            h, b = step % heads, step // heads
            one_head = [(h, pl.ds(pl.multiple_of(h * HD, HD), HD))]
            rows = pl.ds(pl.multiple_of(b * SLOW_ROWS, SLOW_ROWS), SLOW_ROWS)
            row, column = places(b * SLOW_ROWS, (SLOW_ROWS, tokens))
            everyone = column >= jnp.where(odd, 0, tokens)
            for h, lanes in one_head:
                parts = (
                    (ko_ref[:, lanes], vo_ref[:, lanes], column <= row),
                    (ks_ref[:, lanes], vs_ref[:, lanes], everyone),
                )
                values, level = from_maximum(q_ref[rows, lanes], parts)
                out_ref[rows, lanes] = joined(rows, lanes, h, values, level)
            return carry

        lax.fori_loop(0, heads * (tokens // SLOW_ROWS), one_block, 0)

    done = pltpu.make_async_copy(out_ref, out_hbm.at[group], sems.at[9])
    done.start()
    done.wait()


def finish(group, so_far, rank, queries, keys, values, early, far, weights, gain):
    groups, tokens, width = queries.shape
    heads = width // HD
    everywhere = pl.BlockSpec(memory_space=pl.ANY)
    block = pltpu.VMEM((tokens, width), bf16)
    return pl.pallas_call(
        functools.partial(finish_kernel, group),
        out_shape=jax.ShapeDtypeStruct(queries.shape, bf16),
        in_specs=[everywhere, pl.BlockSpec(memory_space=pltpu.SMEM)] + [everywhere] * 9,
        out_specs=everywhere,
        input_output_aliases={0: 0},
        scratch_shapes=[block] * 6
        + [
            pltpu.VMEM((heads, 8, tokens), f32),
            pltpu.VMEM(weights.shape, f32),
            pltpu.VMEM(gain.shape, f32),
            pltpu.VMEM((tokens, width), f32),
            pltpu.VMEM((heads, tokens, 2 * HD), f32),
            block,
            pltpu.SemaphoreType.DMA((10,)),
        ],
        compiler_params=pltpu.CompilerParams(vmem_limit_bytes=VMEM_LIMIT),
        cost_estimate=pl.CostEstimate(
            flops=heads * tokens * tokens * 14 * HD,
            bytes_accessed=16 * tokens * width,
            transcendentals=heads * tokens * 2 * tokens,
        ),
        name="finish",
    )(so_far, rank, queries, keys, values, *early, *far, weights, gain)


def add_kernel(x_ref, out_ref):
    total = jnp.sum(x_ref[...].astype(f32), axis=0).astype(bf16)
    for i in range(out_ref.shape[0]):
        out_ref[i] = total


def after(x, event):
    return lax.optimization_barrier((x, event))[0]


def exchange(tiles):
    return lax.all_to_all(tiles, "seq", 0, 0, tiled=True)


def add_parts(arrived):
    vmem = pl.BlockSpec(memory_space=pltpu.VMEM)
    return pl.pallas_call(
        add_kernel,
        out_shape=jax.ShapeDtypeStruct(arrived.shape, bf16),
        in_specs=[vmem],
        out_specs=vmem,
        compiler_params=pltpu.CompilerParams(vmem_limit_bytes=SMALL_LIMIT),
        name="add_parts",
    )(arrived)


def body(
    query_vectors,
    key_vectors,
    value_vectors,
    token_rates,
    gate_weight,
    up_weight,
    down_weight,
    step_sizes,
    norm_gain,
):
    rank = lax.axis_index("seq")
    size = lax.axis_size("seq")
    gain = norm_gain.reshape(1, -1)
    ranks = rank.astype(jnp.int32).reshape(1)

    def send(block, distance):
        return move(block, lambda i: (i + distance) % size)

    def swap(block):
        return move(block, lambda i: i ^ 1)

    together = lax.optimization_barrier
    first = (gate_weight, up_weight, down_weight)
    own = (query_vectors, key_vectors, value_vectors)
    far_keys = send(key_vectors[0], 2)
    weights, limits, partial = local_grads(
        0, key_vectors, value_vectors, token_rates, first, step_sizes
    )
    far_values = send(after(value_vectors[0], (far_keys, partial)), 2)
    asked = send(after(query_vectors[1], partial), -2)
    early = [swap(t) for t in own[1:]]
    added = add_parts(exchange(partial.reshape(size, -1, HD)))
    summed = exchange(added)
    answer = remote_part(1, size, ranks, after(asked, added), *own[1:], early)
    context = (far_keys, far_values, swap(far_keys), swap(far_values))
    summed, answer = together((summed, answer))
    far = [send(a, 2) for a in answer]
    later = step(summed.reshape(partial.shape), weights, limits)
    (partial,) = local_grads(1, key_vectors, value_vectors, token_rates, (later,))
    arrived = exchange(partial.reshape(size, -1, HD))
    mixed = mix(0, ranks, *own, early, context, weights, gain)
    arrived, mixed = together((arrived, mixed))
    summed = exchange(add_parts(arrived))
    mixed = finish(1, mixed, ranks, *own, early, far, later, gain)
    summed, mixed = together((summed, mixed))
    last = step(summed.reshape(partial.shape), later, limits)
    return mixed, last


def solution(mesh):
    return jax.shard_map(
        body,
        mesh=mesh,
        in_specs=(
            P("batch", "seq", "head"),
            P("batch", "seq", "head"),
            P("batch", "seq", "head"),
            P("batch", "head", "seq"),
            P("head", None, None),
            P("head", None, None),
            P("head", None, None),
            P("head"),
            P("head"),
        ),
        out_specs=(P("batch", "seq", "head"), P("batch", "head", None, None)),
        check_vma=False,
    )
```

```python
import functools
import math

import jax
import jax.numpy as jnp
from jax import lax
from jax.experimental import pallas as pl
from jax.experimental.pallas import tpu as pltpu
from jax.sharding import PartitionSpec as P

HD = 128
FW = 256
NS_STEPS = 5
ROWS = 256
SLOW_ROWS = 128
SLOW_MIX = 64

coeff_first = 3.4445
coeff_second = -4.775
coeff_third = 2.0315
frob_epsilon = 1e-07
rms_epsilon = 1e-06
column_epsilon = 1e-06

f32 = jnp.float32
bf16 = jnp.bfloat16
LEAST_SUM = 1e-25
MOST_SUM = 1e30
NO_KEYS = -1e30
VMEM_LIMIT = 62 * 1024 * 1024
SMALL_LIMIT = 24 * 1024 * 1024
STEP_LIMIT = 24 * 1024 * 1024
PART_LIMIT = 32 * 1024 * 1024


def dot(a, b, over=((1,), (0,))):
    return lax.dot_general(a, b, (over, ((), ())), preferred_element_type=f32)


def sigmoid(x):
    return 0.5 * jnp.tanh(0.5 * x) + 0.5


def move(block, route):
    return lax.ppermute(block, "seq", [(i, route(i)) for i in range(lax.axis_size("seq"))])


def fetch(copies, sems, at=0):
    started = [pltpu.make_async_copy(a, b, sems.at[at + i]) for i, (a, b) in enumerate(copies)]
    for copy in started:
        copy.start()
    return started


def fetch(copies, sems, at=0):
    started = [pltpu.make_async_copy(a, b, sems.at[at + i]) for i, (a, b) in enumerate(copies)]
    for copy in started:
        copy.start()
    return started


def grads_kernel(group, k_ref, v_ref, r_ref, *refs):
    if k_ref.ndim == 3:
        k_ref, v_ref, r_ref = k_ref.at[group], v_ref.at[group], r_ref.at[group]
    *w_refs, out_ref, grad_ref, hid_ref, og_ref = refs
    if len(w_refs) > 1:
        step_ref, *w_refs, kept_ref, limits_ref = w_refs
        for which in range(3):
            weight = w_refs[which][...]
            kept_ref[which] = weight
            limits_ref[which, :, :1] = jnp.sqrt(jnp.sum(weight * weight, axis=1, keepdims=True))
            for h in range(weight.shape[0]):
                limits_ref[which, h, 1:] = jnp.full((1, FW), step_ref[h], f32)
    else:
        w_refs = [w_refs[0].at[which] for which in range(3)]
    tokens, width = k_ref.shape
    for h in range(width // HD):
        lanes = slice(h * HD, (h + 1) * HD)
        low_gate, low_up, low_down = (w_ref[h].astype(bf16) for w_ref in w_refs)
        for c in range(tokens // ROWS):
            rows = slice(c * ROWS, (c + 1) * ROWS)
            keys = k_ref[rows, lanes]
            rate = jnp.broadcast_to(r_ref[h : h + 1, rows], (HD, ROWS)).T
            out_grad = (-rate * v_ref[rows, lanes].astype(f32)).astype(bf16)
            gate_pre = dot(keys, low_gate)
            up_pre = dot(keys, low_up)
            hidden_grad = dot(out_grad, low_down)
            sig = sigmoid(gate_pre)
            active = gate_pre * sig
            og_ref[rows] = out_grad
            hid_ref[rows] = (active * up_pre).astype(bf16)
            grad_ref[rows, FW:] = (hidden_grad * active).astype(bf16)
            grad_ref[rows, :FW] = (
                hidden_grad * up_pre * sig * (1.0 + gate_pre * (1.0 - sig))
            ).astype(bf16)
        both = dot(k_ref[:, lanes], grad_ref[...], ((0,), (0,)))
        down = dot(og_ref[...], hid_ref[...], ((0,), (0,)))
        for which, full in enumerate((both[:, :FW], both[:, FW:], down)):
            for half in range(2):
                out_ref[which, h, half] = full[:, half * HD : (half + 1) * HD].astype(bf16)


def local_grads(group, keys, values, rates, weights, step_sizes=None):
    _, tokens, width = keys.shape
    heads = width // HD
    vmem = pl.BlockSpec(memory_space=pltpu.VMEM)
    out_shape = [jax.ShapeDtypeStruct((3, heads, 2, HD, HD), bf16)]
    if step_sizes is None:
        extra, limit = [], SMALL_LIMIT
        in_specs = [vmem] * (3 + len(weights))
        out_specs = [vmem]
    else:
        extra, limit = [step_sizes], VMEM_LIMIT
        group_rows = pl.BlockSpec((None, tokens, width), lambda i: (group, 0, 0))
        in_specs = (
            [group_rows] * 2
            + [pl.BlockSpec((None, heads, tokens), lambda i: (group, 0, 0))]
            + [pl.BlockSpec(memory_space=pltpu.SMEM)]
            + [pl.BlockSpec((heads, HD, FW), lambda i: (0, 0, 0))] * len(weights)
        )
        out_shape = [
            jax.ShapeDtypeStruct((3, heads, HD, FW), f32),
            jax.ShapeDtypeStruct((3, heads, 2, FW), f32),
        ] + out_shape
        out_specs = [pl.BlockSpec(o.shape, lambda i, n=len(o.shape): (0,) * n) for o in out_shape]
    return pl.pallas_call(
        functools.partial(grads_kernel, group),
        out_shape=out_shape,
        grid=(1,) if extra else (),
        in_specs=in_specs,
        out_specs=out_specs,
        scratch_shapes=[
            pltpu.VMEM((tokens, 2 * FW), bf16),
            pltpu.VMEM((tokens, FW), bf16),
            pltpu.VMEM((tokens, HD), bf16),
        ],
        compiler_params=pltpu.CompilerParams(vmem_limit_bytes=limit),
        cost_estimate=pl.CostEstimate(
            flops=12 * heads * tokens * HD * FW,
            bytes_accessed=4 * tokens * width,
            transcendentals=heads * tokens * FW,
        ),
        name="local_grads",
    )(keys, values, rates, *extra, *weights)


def split(x):
    high = x.astype(bf16)
    return high, (x - high.astype(f32)).astype(bf16)


def sweeps(x_ref, count):
    def sweep(_, carry):
        pieces, grams, polynomials = [], [], []
        for m in range(count):
            high, low = split(x_ref[m])
            pieces.append((high, low))
            stacked = jnp.concatenate([high, low], axis=0)
            g = dot(stacked, stacked, ((1,), (1,)))
            grams.append(g[:HD, :HD] + (g[HD:, :HD] + g[:HD, HD:]) + g[HD:, HD:])
        for m in range(count):
            row = jnp.concatenate(split(grams[m]), axis=1)
            squared = dot(row, jnp.concatenate([row, row], axis=0))
            polynomials.append(
                coeff_second * grams[m] + coeff_third * (squared[:, :HD] + squared[:, HD:])
            )
        for m in range(count):
            high, low = pieces[m]
            row = jnp.concatenate(split(polynomials[m]), axis=1)
            product = dot(row, jnp.concatenate([high, high], axis=0)) + dot(
                row, jnp.concatenate([low, low], axis=0)
            )
            x_ref[m] = coeff_first * x_ref[m] + product
        return carry

    lax.fori_loop(0, NS_STEPS, sweep, 0)


def step_kernel(s_ref, w_hbm, limits_hbm, out_hbm, x_ref, w_ref, limits_ref, out_ref, sems):
    heads = out_ref.shape[1]
    started = fetch([(w_hbm, w_ref), (limits_hbm, limits_ref)], sems)
    for which in range(3):
        for h in range(heads):
            grad = jnp.concatenate([s_ref[which, h, 0], s_ref[which, h, 1]], axis=1).astype(f32)
            frobenius = jnp.sqrt(jnp.sum(grad * grad, keepdims=True))
            x_ref[which * heads + h] = grad / (frobenius + frob_epsilon)
    sweeps(x_ref, 3 * heads)
    for copy in started:
        copy.wait()
    written = []
    for which in range(3):
        for h in range(heads):
            target = limits_ref[which, h, :1]
            stepped = w_ref[which, h] - limits_ref[which, h, 1:] * x_ref[which * heads + h]
            length = jnp.sqrt(jnp.sum(stepped * stepped, axis=0, keepdims=True))
            out_ref[which, h] = stepped * (target / (length + column_epsilon))
        copy = pltpu.make_async_copy(out_ref.at[which], out_hbm.at[which], sems.at[2 + which])
        copy.start()
        written.append(copy)
    for copy in written:
        copy.wait()


def step(summed, weights, limits):
    heads = weights.shape[1]
    everywhere = pl.BlockSpec(memory_space=pl.ANY)
    return pl.pallas_call(
        step_kernel,
        out_shape=jax.ShapeDtypeStruct(weights.shape, f32),
        in_specs=[pl.BlockSpec(memory_space=pltpu.VMEM), everywhere, everywhere],
        out_specs=everywhere,
        scratch_shapes=[
            pltpu.VMEM((3 * heads, HD, FW), f32),
            pltpu.VMEM(weights.shape, f32),
            pltpu.VMEM(limits.shape, f32),
            pltpu.VMEM(weights.shape, f32),
            pltpu.SemaphoreType.DMA((5,)),
        ],
        compiler_params=pltpu.CompilerParams(vmem_limit_bytes=STEP_LIMIT),
        cost_estimate=pl.CostEstimate(
            flops=3 * heads * NS_STEPS * 40 * HD * HD * FW,
            bytes_accessed=3 * heads * 10 * HD * FW,
            transcendentals=0,
        ),
        name="weight_step",
    )(summed, weights, limits)


def mix_kernel(group, rank_ref, *refs):
    (
        q_hbm, k_hbm, v_hbm, ks_hbm, vs_hbm, kf_hbm, vf_hbm, kb_hbm, vb_hbm, w_hbm, gain_hbm,
        out_hbm, q_ref, ko_ref, vo_ref, kf_ref, vf_ref, kn_ref, vn_ref, w_ref, gain_ref,
        normed_ref, out_ref, sems,
    ) = refs
    tokens, width = q_ref.shape
    heads = width // HD
    scale = 1.0 / math.sqrt(HD)
    power = scale * math.log2(math.e)
    blocks = tokens // ROWS
    odd = rank_ref[0] % 2 == 1
    started = fetch(
        [
            (w_hbm, w_ref),
            (gain_hbm, gain_ref),
            (q_hbm.at[group], q_ref),
            (k_hbm.at[group], ko_ref),
            (v_hbm.at[group], vo_ref),
            (kf_hbm, kf_ref),
            (vf_hbm, vf_ref),
        ],
        sems,
    )
    beside = [(ks_hbm.at[group], kn_ref), (vs_hbm.at[group], vn_ref)]
    behind = [(kb_hbm, kn_ref), (vb_hbm, vn_ref)]

    @pl.when(odd)
    def _():
        fetch(beside, sems, 7)

    @pl.when(jnp.logical_not(odd))
    def _():
        fetch(behind, sems, 7)

    started += [pltpu.make_async_copy(a, b, sems.at[7 + i]) for i, (a, b) in enumerate(behind)]
    for copy in started[:3]:
        copy.wait()
    all_lanes = [slice(h * HD, (h + 1) * HD) for h in range(heads)]
    all_rows = [slice(b * ROWS, (b + 1) * ROWS) for b in range(blocks)]
    for h, lanes in enumerate(all_lanes):
        low_gate, low_up, low_down = (w_ref[which, h].astype(bf16) for which in range(3))
        for rows in all_rows:
            q = q_ref[rows, lanes]
            gate_pre = dot(q, low_gate)
            hidden = (gate_pre * sigmoid(gate_pre) * dot(q, low_up)).astype(bf16)
            applied = dot(hidden, low_down, ((1,), (1,)))
            mean = jnp.mean(applied * applied, axis=1, keepdims=True)
            normed_ref[rows, lanes] = applied * lax.rsqrt(mean + rms_epsilon) * gain_ref[:, lanes]
    for copy in started[3:]:
        copy.wait()

    near_valid = rank_ref[0] >= 1 if group == 0 else True
    far_valid = rank_ref[0] >= 2 if group == 0 else True

    def beside_ones(v, valid=True):
        wide = jnp.concatenate([v, jnp.ones((v.shape[0], HD), bf16)], axis=1)
        return wide if valid is True else wide * jnp.where(valid, 1.0, 0.0).astype(bf16)

    causal = lax.broadcasted_iota(jnp.int32, (ROWS, ROWS), 0) >= lax.broadcasted_iota(
        jnp.int32, (ROWS, ROWS), 1
    )

    def raised(q, keys):
        return jnp.exp2(dot(q, keys, ((1,), (1,))) * power).astype(bf16)

    wrong = jnp.zeros((ROWS, HD), f32)
    for lanes in all_lanes:
        for b, rows in enumerate(all_rows):
            q = q_ref[rows, lanes]
            own = dot(q, ko_ref[rows, lanes], ((1,), (1,)))
            far = dot(q, kf_ref[rows, lanes], ((1,), (1,)))
            edge = jnp.exp2(jnp.where(causal, own, far) * power)
            total = dot(
                jnp.where(causal, edge, 0.0).astype(bf16), beside_ones(vo_ref[rows, lanes])
            )
            total += dot(
                jnp.where(causal, 0.0, edge).astype(bf16),
                beside_ones(vf_ref[rows, lanes], far_valid),
            )
            total += dot(raised(q, kn_ref[:, lanes]), beside_ones(vn_ref[:, lanes], near_valid))
            if b > 0:
                past = slice(0, b * ROWS)
                total += dot(raised(q, ko_ref[past, lanes]), beside_ones(vo_ref[past, lanes]))
            if b < blocks - 1:
                rest = slice((b + 1) * ROWS, tokens)
                total += dot(
                    raised(q, kf_ref[rest, lanes]), beside_ones(vf_ref[rest, lanes], far_valid)
                )
            sums = total[:, HD:]
            out_ref[rows, lanes] = (normed_ref[rows, lanes] + total[:, :HD] / sums).astype(bf16)
            fine = (sums > LEAST_SUM) & (sums < MOST_SUM)
            wrong = jnp.maximum(wrong, jnp.where(fine, 0.0, 1.0))

    @pl.when(jnp.max(wrong) > 0.0)
    def _():
        def one_block(step, carry):
            h, b = step % heads, step // heads
            one_head = [pl.ds(pl.multiple_of(h * HD, HD), HD)]
            rows = pl.ds(pl.multiple_of(b * SLOW_MIX, SLOW_MIX), SLOW_MIX)
            place, column = places(b * SLOW_MIX, (SLOW_MIX, tokens))
            limit = jnp.where(far_valid, tokens, -1)
            least = jnp.where(near_valid, 0, tokens)
            lowest = jnp.float32(-jnp.inf)
            for lanes in one_head:
                q = q_ref[rows, lanes]
                far = dot(q, kf_ref[:, lanes], ((1,), (1,))) * scale
                far = jnp.where((column > place) & (column < limit), far, lowest)
                near = dot(q, kn_ref[:, lanes], ((1,), (1,))) * scale
                near = jnp.where(column >= least, near, lowest)
                own = dot(q, ko_ref[:, lanes], ((1,), (1,))) * scale
                own = jnp.where(column <= place, own, lowest)
                parts = ((far, vf_ref), (near, vn_ref), (own, vo_ref))
                most = jnp.max(own, axis=1, keepdims=True)
                for scores, _ in parts[:2]:
                    most = jnp.maximum(most, jnp.max(scores, axis=1, keepdims=True))
                total = jnp.zeros((SLOW_MIX, HD), f32)
                sums = jnp.zeros((SLOW_MIX, 1), f32)
                for scores, v_ref in parts:
                    e = jnp.exp(scores - most)
                    sums += jnp.sum(e, axis=1, keepdims=True)
                    total += dot(e.astype(bf16), v_ref[:, lanes])
                out_ref[rows, lanes] = (normed_ref[rows, lanes] + total / sums).astype(bf16)
            return carry

        lax.fori_loop(0, heads * (tokens // SLOW_MIX), one_block, 0)

    done = pltpu.make_async_copy(out_ref, out_hbm.at[group], sems.at[9])
    done.start()
    done.wait()


def mix(group, rank, queries, keys, values, early, context, weights, gain):
    groups, tokens, width = queries.shape
    heads = width // HD
    everywhere = pl.BlockSpec(memory_space=pl.ANY)
    block = pltpu.VMEM((tokens, width), bf16)
    return pl.pallas_call(
        functools.partial(mix_kernel, group),
        out_shape=jax.ShapeDtypeStruct(queries.shape, bf16),
        in_specs=[pl.BlockSpec(memory_space=pltpu.SMEM)] + [everywhere] * 11,
        out_specs=everywhere,
        scratch_shapes=[block] * 7
        + [
            pltpu.VMEM(weights.shape, f32),
            pltpu.VMEM(gain.shape, f32),
            pltpu.VMEM((tokens, width), f32),
            block,
            pltpu.SemaphoreType.DMA((10,)),
        ],
        compiler_params=pltpu.CompilerParams(vmem_limit_bytes=VMEM_LIMIT),
        cost_estimate=pl.CostEstimate(
            flops=heads * tokens * 2 * tokens * 8 * HD,
            bytes_accessed=16 * tokens * width,
            transcendentals=heads * tokens * 2 * tokens,
        ),
        name="mix",
    )(rank, queries, keys, values, *early, *context, weights, gain)


def raise_to(q, keys):
    power = math.log2(math.e) / math.sqrt(HD)
    return jnp.exp2(dot(q, keys, ((1,), (1,))) * power)


def with_ones(v):
    return jnp.concatenate([v, jnp.ones((v.shape[0], HD), bf16)], axis=1)


def weighted(e, v):
    return dot(e.astype(bf16), with_ones(v))


def from_maximum(q, parts):
    scores = []
    most = jnp.full((q.shape[0], 1), NO_KEYS, f32)
    for keys, _, allowed in parts:
        s = dot(q, keys, ((1,), (1,))) / math.sqrt(HD)
        scores.append(s)
        most = jnp.maximum(
            most, jnp.max(jnp.where(allowed, s, NO_KEYS), axis=1, keepdims=True)
        )
    total = jnp.zeros((q.shape[0], HD), f32)
    sums = jnp.zeros((q.shape[0], 1), f32)
    for s, (_, values, allowed) in zip(scores, parts):
        e = jnp.where(allowed, jnp.exp(jnp.where(allowed, s, most) - most), 0.0)
        sums += jnp.sum(e, axis=1, keepdims=True)
        total += dot(e.astype(bf16), values)
    some = sums > 0.0
    safe = jnp.where(some, sums, 1.0)
    level = jnp.where(some, most + jnp.log(safe), NO_KEYS)
    return total / safe, jnp.broadcast_to(level, total.shape)


def unsafe(sums):
    return jnp.where((sums > LEAST_SUM) & (sums < MOST_SUM), 0.0, 1.0)


def places(first_row, shape):
    row = first_row + lax.broadcasted_iota(jnp.int32, shape, 0)
    return row, lax.broadcasted_iota(jnp.int32, shape, 1)


def remote_kernel(group, size, rank_ref, *refs):
    (
        q_hbm, k_hbm, v_hbm, ks_hbm, vs_hbm, out_ref, level_ref,
        q_ref, ko_ref, vo_ref, ks_ref, vs_ref, total_ref, sems,
    ) = refs
    tokens, width = q_ref.shape
    heads = width // HD
    blocks = tokens // ROWS
    rank = rank_ref[0]
    even = rank % 2 == 0
    at = jnp.where(rank >= size - 2, group - 1, group)
    started = fetch(
        [
            (q_hbm, q_ref),
            (k_hbm.at[at], ko_ref),
            (v_hbm.at[at], vo_ref),
            (ks_hbm.at[at], ks_ref),
            (vs_hbm.at[at], vs_ref),
        ],
        sems,
    )
    for copy in started[:3]:
        copy.wait()
    all_lanes = [slice(h * HD, (h + 1) * HD) for h in range(heads)]
    all_rows = [slice(b * ROWS, (b + 1) * ROWS) for b in range(blocks)]
    row, column = places(0, (ROWS, ROWS))
    for h, lanes in enumerate(all_lanes):
        for b, rows in enumerate(all_rows):
            q = q_ref[rows, lanes]
            e = jnp.where(column > row, raise_to(q, ko_ref[rows, lanes]), 0.0)
            total = weighted(e, vo_ref[rows, lanes])
            if b < blocks - 1:
                rest = slice((b + 1) * ROWS, tokens)
                total += weighted(raise_to(q, ko_ref[rest, lanes]), vo_ref[rest, lanes])
            total_ref[h, rows] = total
    for copy in started[3:]:
        copy.wait()

    @pl.when(even)
    def _():
        for h, lanes in enumerate(all_lanes):
            for rows in all_rows:
                e = raise_to(q_ref[rows, lanes], ks_ref[:, lanes])
                total_ref[h, rows] += weighted(e, vs_ref[:, lanes])

    wrong = jnp.zeros((ROWS, HD), f32)
    for h, lanes in enumerate(all_lanes):
        for b, rows in enumerate(all_rows):
            total = total_ref[h, rows]
            sums = total[:, HD:]
            some = sums > 0.0
            safe = jnp.where(some, sums, 1.0)
            out_ref[rows, lanes] = (total[:, :HD] / safe).astype(bf16)
            level = jnp.where(some, jnp.log(safe), NO_KEYS)
            level_ref[h, :, rows] = level.T[:8]
            bad = unsafe(sums)
            if b == blocks - 1:
                last = lax.broadcasted_iota(jnp.int32, bad.shape, 0) == ROWS - 1
                bad = jnp.where(last & jnp.logical_not(even), 0.0, bad)
            wrong = jnp.maximum(wrong, bad)

    @pl.when(jnp.max(wrong) > 0.0)
    def _():
        def one_block(step, carry):
            h, b = step % heads, step // heads
            one_head = [(h, pl.ds(pl.multiple_of(h * HD, HD), HD))]
            rows = pl.ds(pl.multiple_of(b * SLOW_ROWS, SLOW_ROWS), SLOW_ROWS)
            row, column = places(b * SLOW_ROWS, (SLOW_ROWS, tokens))
            everyone = column >= jnp.where(even, 0, tokens)
            for h, lanes in one_head:
                parts = (
                    (ko_ref[:, lanes], vo_ref[:, lanes], column > row),
                    (ks_ref[:, lanes], vs_ref[:, lanes], everyone),
                )
                values, level = from_maximum(q_ref[rows, lanes], parts)
                out_ref[rows, lanes] = values.astype(bf16)
                level_ref[h, :, rows] = level.T[:8]
            return carry

        lax.fori_loop(0, heads * (tokens // SLOW_ROWS), one_block, 0)


def remote_part(group, size, rank, received, keys, values, early):
    tokens, width = received.shape
    heads = width // HD
    everywhere = pl.BlockSpec(memory_space=pl.ANY)
    block = pltpu.VMEM((tokens, width), bf16)
    return pl.pallas_call(
        functools.partial(remote_kernel, group, size),
        out_shape=[
            jax.ShapeDtypeStruct((tokens, width), bf16),
            jax.ShapeDtypeStruct((heads, 8, tokens), f32),
        ],
        in_specs=[pl.BlockSpec(memory_space=pltpu.SMEM)] + [everywhere] * 5,
        out_specs=[pl.BlockSpec()] * 2,
        scratch_shapes=[block] * 5
        + [pltpu.VMEM((heads, tokens, 2 * HD), f32), pltpu.SemaphoreType.DMA((5,))],
        compiler_params=pltpu.CompilerParams(vmem_limit_bytes=PART_LIMIT),
        cost_estimate=pl.CostEstimate(
            flops=heads * tokens * tokens * 8 * HD,
            bytes_accessed=12 * tokens * width,
            transcendentals=heads * tokens * tokens,
        ),
        name="remote_part",
    )(rank, received, keys, values, *early)


def finish_kernel(group, _, rank_ref, *refs):
    (
        q_hbm, k_hbm, v_hbm, ks_hbm, vs_hbm, o_hbm, level_hbm, w_hbm, gain_hbm, out_hbm,
        q_ref, ko_ref, vo_ref, ks_ref, vs_ref, o_ref, level_ref, w_ref, gain_ref,
        normed_ref, total_ref, out_ref, sems,
    ) = refs
    tokens, width = q_ref.shape
    heads = width // HD
    blocks = tokens // ROWS
    odd = rank_ref[0] % 2 == 1
    started = fetch(
        [
            (w_hbm, w_ref),
            (gain_hbm, gain_ref),
            (q_hbm.at[group], q_ref),
            (k_hbm.at[group], ko_ref),
            (v_hbm.at[group], vo_ref),
            (ks_hbm.at[group], ks_ref),
            (vs_hbm.at[group], vs_ref),
            (o_hbm, o_ref),
            (level_hbm, level_ref),
        ],
        sems,
    )
    for copy in started[:3]:
        copy.wait()
    all_lanes = [slice(h * HD, (h + 1) * HD) for h in range(heads)]
    all_rows = [slice(b * ROWS, (b + 1) * ROWS) for b in range(blocks)]
    for h, lanes in enumerate(all_lanes):
        low_gate, low_up, low_down = (w_ref[which, h].astype(bf16) for which in range(3))
        for rows in all_rows:
            q = q_ref[rows, lanes]
            gate_pre = dot(q, low_gate)
            hidden = (gate_pre * sigmoid(gate_pre) * dot(q, low_up)).astype(bf16)
            applied = dot(hidden, low_down, ((1,), (1,)))
            mean = jnp.mean(applied * applied, axis=1, keepdims=True)
            normed_ref[rows, lanes] = applied * lax.rsqrt(mean + rms_epsilon) * gain_ref[:, lanes]
    for copy in started[3:]:
        copy.wait()
    row, column = places(0, (ROWS, ROWS))
    for h, lanes in enumerate(all_lanes):
        for b, rows in enumerate(all_rows):
            q = q_ref[rows, lanes]
            e = jnp.where(column <= row, raise_to(q, ko_ref[rows, lanes]), 0.0)
            total = weighted(e, vo_ref[rows, lanes])
            if b > 0:
                past = slice(0, b * ROWS)
                total += weighted(raise_to(q, ko_ref[past, lanes]), vo_ref[past, lanes])
            total_ref[h, rows] = total

    @pl.when(odd)
    def _():
        for h, lanes in enumerate(all_lanes):
            for rows in all_rows:
                e = raise_to(q_ref[rows, lanes], ks_ref[:, lanes])
                total_ref[h, rows] += weighted(e, vs_ref[:, lanes])

    def joined(rows, lanes, h, values, level):
        other = jnp.broadcast_to(level_ref[h, :1, rows], (HD, values.shape[0])).T
        share = sigmoid(other - level)
        attended = values + share * (o_ref[rows, lanes].astype(f32) - values)
        return (normed_ref[rows, lanes] + attended).astype(bf16)

    wrong = jnp.zeros((ROWS, HD), f32)
    for h, lanes in enumerate(all_lanes):
        for rows in all_rows:
            total = total_ref[h, rows]
            sums = total[:, HD:]
            out_ref[rows, lanes] = joined(rows, lanes, h, total[:, :HD] / sums, jnp.log(sums))
            wrong = jnp.maximum(wrong, unsafe(sums))

    @pl.when(jnp.max(wrong) > 0.0)
    def _():
        def one_block(step, carry):
            h, b = step % heads, step // heads
            one_head = [(h, pl.ds(pl.multiple_of(h * HD, HD), HD))]
            rows = pl.ds(pl.multiple_of(b * SLOW_ROWS, SLOW_ROWS), SLOW_ROWS)
            row, column = places(b * SLOW_ROWS, (SLOW_ROWS, tokens))
            everyone = column >= jnp.where(odd, 0, tokens)
            for h, lanes in one_head:
                parts = (
                    (ko_ref[:, lanes], vo_ref[:, lanes], column <= row),
                    (ks_ref[:, lanes], vs_ref[:, lanes], everyone),
                )
                values, level = from_maximum(q_ref[rows, lanes], parts)
                out_ref[rows, lanes] = joined(rows, lanes, h, values, level)
            return carry

        lax.fori_loop(0, heads * (tokens // SLOW_ROWS), one_block, 0)

    done = pltpu.make_async_copy(out_ref, out_hbm.at[group], sems.at[9])
    done.start()
    done.wait()


def finish(group, so_far, rank, queries, keys, values, early, far, weights, gain):
    groups, tokens, width = queries.shape
    heads = width // HD
    everywhere = pl.BlockSpec(memory_space=pl.ANY)
    block = pltpu.VMEM((tokens, width), bf16)
    return pl.pallas_call(
        functools.partial(finish_kernel, group),
        out_shape=jax.ShapeDtypeStruct(queries.shape, bf16),
        in_specs=[everywhere, pl.BlockSpec(memory_space=pltpu.SMEM)] + [everywhere] * 9,
        out_specs=everywhere,
        input_output_aliases={0: 0},
        scratch_shapes=[block] * 6
        + [
            pltpu.VMEM((heads, 8, tokens), f32),
            pltpu.VMEM(weights.shape, f32),
            pltpu.VMEM(gain.shape, f32),
            pltpu.VMEM((tokens, width), f32),
            pltpu.VMEM((heads, tokens, 2 * HD), f32),
            block,
            pltpu.SemaphoreType.DMA((10,)),
        ],
        compiler_params=pltpu.CompilerParams(vmem_limit_bytes=VMEM_LIMIT),
        cost_estimate=pl.CostEstimate(
            flops=heads * tokens * tokens * 14 * HD,
            bytes_accessed=16 * tokens * width,
            transcendentals=heads * tokens * 2 * tokens,
        ),
        name="finish",
    )(so_far, rank, queries, keys, values, *early, *far, weights, gain)


def add_kernel(x_ref, out_ref):
    total = jnp.sum(x_ref[...].astype(f32), axis=0).astype(bf16)
    for i in range(out_ref.shape[0]):
        out_ref[i] = total


def after(x, event):
    return lax.optimization_barrier((x, event))[0]


def exchange(tiles):
    return lax.all_to_all(tiles, "seq", 0, 0, tiled=True)


def add_parts(arrived):
    vmem = pl.BlockSpec(memory_space=pltpu.VMEM)
    return pl.pallas_call(
        add_kernel,
        out_shape=jax.ShapeDtypeStruct(arrived.shape, bf16),
        in_specs=[vmem],
        out_specs=vmem,
        compiler_params=pltpu.CompilerParams(vmem_limit_bytes=SMALL_LIMIT),
        name="add_parts",
    )(arrived)


def body(
    query_vectors,
    key_vectors,
    value_vectors,
    token_rates,
    gate_weight,
    up_weight,
    down_weight,
    step_sizes,
    norm_gain,
):
    rank = lax.axis_index("seq")
    size = lax.axis_size("seq")
    gain = norm_gain.reshape(1, -1)
    ranks = rank.astype(jnp.int32).reshape(1)

    def send(block, distance):
        return move(block, lambda i: (i + distance) % size)

    def swap(block):
        return move(block, lambda i: i ^ 1)

    together = lax.optimization_barrier
    first = (gate_weight, up_weight, down_weight)
    own = (query_vectors, key_vectors, value_vectors)
    far_keys = send(key_vectors[0], 2)
    weights, limits, partial = local_grads(
        0, key_vectors, value_vectors, token_rates, first, step_sizes
    )
    far_values = send(after(value_vectors[0], (far_keys, partial)), 2)
    asked = send(query_vectors[1], -2)
    early = [swap(t) for t in own[1:]]
    added = add_parts(exchange(partial.reshape(size, -1, HD)))
    summed = exchange(added)
    answer = remote_part(1, size, ranks, after(asked, added), *own[1:], early)
    context = (far_keys, far_values, swap(far_keys), swap(far_values))
    summed, answer = together((summed, answer))
    far = [send(a, 2) for a in answer]
    later = step(summed.reshape(partial.shape), weights, limits)
    (partial,) = local_grads(1, key_vectors, value_vectors, token_rates, (later,))
    arrived = exchange(partial.reshape(size, -1, HD))
    mixed = mix(0, ranks, *own, early, context, weights, gain)
    arrived, mixed = together((arrived, mixed))
    summed = exchange(add_parts(arrived))
    mixed = finish(1, mixed, ranks, *own, early, far, later, gain)
    summed, mixed = together((summed, mixed))
    last = step(summed.reshape(partial.shape), later, limits)
    return mixed, last


def solution(mesh):
    return jax.shard_map(
        body,
        mesh=mesh,
        in_specs=(
            P("batch", "seq", "head"),
            P("batch", "seq", "head"),
            P("batch", "seq", "head"),
            P("batch", "head", "seq"),
            P("head", None, None),
            P("head", None, None),
            P("head", None, None),
            P("head"),
            P("head"),
        ),
        out_specs=(P("batch", "seq", "head"), P("batch", "head", None, None)),
        check_vma=False,
    )
```
